512 devices in a mesh: dp: 64 (over y, x, core), mp: 8 (over z).
Axes of the slice: x: 4, y: 8, z: 8, core: 2. Of those that a mesh axis runs over, the one named last changes fastest.
Arguments:
- partial_grads: bfloat16 [64, 2, 2, 512, 4096], P('dp', None, None, None, 'mp')
- factors: bfloat16 [8, 8, 512, 1024], P('mp', None, 'dp'), as said below
- inverse_factors: bfloat16 [8, 8, 512, 1024], P('mp', None, 'dp'), as said below
- probes: bfloat16 [8, 8, 512, 512], P('mp', None, 'dp'), may hold values from -6 to 6
- slot_table: int32 [8, 4], P('mp'), may hold values from 0 to 7, as said below
Outputs:
- preconditioned: bfloat16 [2, 2, 512, 4096], P(None, None, 'dp', 'mp')
- new_factors: bfloat16 [8, 8, 512, 1024], P('mp', None, 'dp')
The draws below stay inside these ranges and needn't reach their ends.
Inputs may be any that keep to these rules, and one draw needn't show every extreme that they name: `slot_table`: in each row the 4 entries are distinct slots; slot j belongs to owner j // 2 (an owner is a group of 16 consecutive dp devices; the starting program sends slots 2k and 2k+1 to dp device 16k for updating), and in every row some owner holds 2 blocks. `factors`: both halves of every slot are upper triangular with a positive diagonal. `inverse_factors`: both halves of every slot are upper triangular with a positive diagonal.
All inputs are finite; a program needn't handle non-finite values. Where the reference program divides by a largest or mean magnitude, that divisor is 1e-20 or more.
Results may differ from the reference program's by a relative error of at most 0.011.
Values may be sent and summed in bfloat16 or wider, within the bound.
A program may use at most 64 MiB of HBM per device.

```python
import math
import jax
import jax.numpy as jnp
from jax import lax

BLOCK = 512
EXPERTS = 2
BROW = 2
GROUP = 16
BLK_COL = 4
SLOTS = 2
OWN_SLOTS = 8
WCOLS = 4096
N_DP = 64
N_MP = 8


def draw_partial_grads(key, part):
    full_shape = (N_DP, EXPERTS, BROW, BLOCK, WCOLS)
    noise_key = jax.random.fold_in(key, 11)
    row_key = jax.random.fold_in(key, 12)
    col_key = jax.random.fold_in(key, 13)
    row_index = jnp.arange(BLOCK, dtype=jnp.float32)
    rise_scale = jnp.exp(0.55 * row_index / BLOCK)
    row_scale = jnp.exp(jax.random.uniform(row_key, (EXPERTS, BROW, BLOCK), minval=0.0, maxval=math.log(10.0))) * rise_scale
    col_scale = jnp.exp(jax.random.uniform(col_key, (WCOLS,), minval=0.0, maxval=math.log(4.0)))
    values = jax.random.normal(noise_key, full_shape)
    scaled = 0.25 * values * row_scale[None, :, :, :, None] * col_scale
    return scaled.astype(jnp.float32).astype(jnp.bfloat16)


def triangular_draw(key, first_tag, second_tag):
    full_shape = (N_MP, OWN_SLOTS, 2, BLOCK, BLOCK)
    diag_key = jax.random.fold_in(key, first_tag)
    upper_key = jax.random.fold_in(key, second_tag)
    diag_values = jnp.exp(jax.random.uniform(diag_key, full_shape[:-1], minval=math.log(0.7), maxval=math.log(1.4)))
    upper_values = jax.random.normal(upper_key, full_shape)
    row_index = jnp.arange(BLOCK)[:, None]
    col_index = jnp.arange(BLOCK)[None, :]
    upper_mask = col_index > row_index
    eye_mask = col_index == row_index
    matrix = jnp.where(upper_mask, upper_values * (0.35 / math.sqrt(BLOCK)), 0.0)
    matrix = matrix + jnp.where(eye_mask, diag_values[..., :, None], 0.0)
    matrix = matrix.transpose(0, 1, 3, 2, 4).reshape(N_MP, OWN_SLOTS, BLOCK, 2 * BLOCK)
    return matrix.astype(jnp.float32).astype(jnp.bfloat16)


def draw_factors(key, part):
    return triangular_draw(key, 21, 22)


def draw_inverse_factors(key, part):
    return triangular_draw(key, 31, 32)


def draw_slot_table(key, part):
    owners = N_DP // GROUP
    rest_count = BLK_COL - SLOTS

    def one_column(col_key):
        first_key = jax.random.fold_in(col_key, 1)
        second_key = jax.random.fold_in(col_key, 2)
        third_key = jax.random.fold_in(col_key, 3)
        fourth_key = jax.random.fold_in(col_key, 4)
        owner_order = jax.random.permutation(first_key, owners)
        busy_slots = owner_order[0] * SLOTS + jax.random.permutation(second_key, SLOTS)
        extra_slots = owner_order[1:1 + rest_count] * SLOTS + jax.random.randint(third_key, (rest_count,), 0, SLOTS)
        listed = jnp.concatenate([busy_slots, extra_slots]).astype(jnp.int32)
        shuffle = jax.random.permutation(fourth_key, BLK_COL)
        return jnp.zeros((BLK_COL,), jnp.int32).at[shuffle].set(listed)
    column_keys = jax.vmap(lambda index_value: jax.random.fold_in(key, index_value))(jnp.arange(N_MP))
    return jax.vmap(one_column)(column_keys)


def block_scale(key, dims, split, low, largest):
    factor_of, own = 1.0, jax.random.fold_in(key, 6)
    for position, parts in split:
        draws = jnp.exp(jax.random.uniform(jax.random.fold_in(own, position), (parts,), jnp.float32, low / len(split), largest / len(split)))
        factor_of = factor_of * jnp.repeat(draws, dims[position] // parts).reshape([-1 if axis == position else 1 for axis in range(len(dims))])
    return factor_of


def normal_values(rng, extent, deviation, reach, cuts=(), kind=jnp.bfloat16):
    array = deviation * jax.random.normal(rng, extent, jnp.float32)
    if cuts:
        array = array * block_scale(rng, extent, cuts, -0.22, 0.18)
    return jnp.clip(array, -reach, reach).astype(kind)


def setup_inputs(seed: int = 0) -> dict:
    keys = jax.random.split(jax.random.key(seed), 6)
    return {
        "partial_grads": draw_partial_grads(jax.random.fold_in(keys[5], 71), 0),
        "factors": draw_factors(jax.random.fold_in(keys[5], 71), 0),
        "inverse_factors": draw_inverse_factors(jax.random.fold_in(keys[5], 71), 0),
        "probes": normal_values(keys[3], (N_MP, OWN_SLOTS, BLOCK, BLOCK), 1.0, 6.0, ((0, 8), (2, 64))),
        "slot_table": draw_slot_table(jax.random.fold_in(keys[5], 71), 0),
    }


CLIP_RMS = 0.3
LEARN_RATE = 0.1
EPS_NORM = 1e-06

def product(left_op, right_op):
    return jnp.dot(left_op.astype(jnp.float32), right_op.astype(jnp.float32), precision=lax.Precision.HIGHEST)

def step_factor(factor, first_gram, second_gram):
    bound_value = jnp.max(jnp.abs(first_gram + second_gram)) + EPS_NORM
    change = jnp.triu(first_gram - second_gram).astype(jnp.bfloat16)
    moved_rows = product(change, factor)
    return (factor.astype(jnp.float32) - LEARN_RATE / bound_value * moved_rows).astype(jnp.bfloat16)

def update_block(gradient, left_q, right_q, left_inv, right_inv, probe_mat):
    left_times = product(left_q, gradient).astype(jnp.bfloat16)
    whitened = product(left_times, right_q.T).astype(jnp.bfloat16)
    half_conjugate = product(left_inv.T, probe_mat).astype(jnp.bfloat16)
    conjugate = product(half_conjugate, right_inv).astype(jnp.bfloat16)
    new_left = step_factor(left_q, product(whitened, whitened.T), product(conjugate, conjugate.T))
    new_right = step_factor(right_q, product(whitened.T, whitened), product(conjugate.T, conjugate))
    precond_left = product(new_left.T, new_left).astype(jnp.bfloat16)
    precond_right = product(new_right.T, new_right).astype(jnp.bfloat16)
    middle = product(precond_left, gradient).astype(jnp.bfloat16)
    result = product(middle, precond_right).astype(jnp.bfloat16)
    return (result, jnp.concatenate([new_left, new_right], axis=1))

def run_one(item_set):
    state = item_set[1]
    return update_block(item_set[0], state[:, :BLOCK], state[:, BLOCK:2 * BLOCK], state[:, 2 * BLOCK:3 * BLOCK], state[:, 3 * BLOCK:], item_set[2])

def reference(partial_grads, factors, inverse_factors, probes, slot_table):

    def accumulate(running, piece_dp):
        return (running + piece_dp.astype(jnp.float32), None)
    summed, _ = lax.scan(accumulate, jnp.zeros(partial_grads.shape[1:], jnp.float32), partial_grads)
    entry_count = EXPERTS * BROW * BLOCK * WCOLS
    squares = jnp.sum(summed * summed)
    clip_factor = jnp.minimum(1.0, CLIP_RMS * math.sqrt(entry_count) / jnp.sqrt(squares + EPS_NORM))
    clipped = (summed * clip_factor).astype(jnp.bfloat16)
    blocks = clipped.reshape(BLK_COL, BLOCK, N_MP, BLOCK).transpose(2, 0, 1, 3)
    results = []
    states = []
    for column in range(N_MP):
        table_row = slot_table[column].astype(jnp.int32)
        state_col = factors[column]
        combined = jnp.concatenate([state_col, inverse_factors[column]], axis=2)
        chosen = combined[table_row]
        chosen_probe = probes[column][table_row]
        block_out, factor_out = lax.map(run_one, (blocks[column], chosen, chosen_probe))
        results.append(block_out)
        states.append(state_col.at[table_row].set(factor_out))
    preconditioned = jnp.stack(results).transpose(1, 2, 0, 3).reshape(EXPERTS, BROW, BLOCK, WCOLS)
    return (preconditioned, jnp.stack(states))
```

```python
import functools
import math

import jax
import jax.numpy as jnp
from jax import lax
from jax.experimental import pallas as pl
from jax.experimental.pallas import tpu as pltpu
from jax.sharding import PartitionSpec as P

CLIP_RMS = 0.3
LEARN_RATE = 0.1
EPS_NORM = 1e-06

NX, NY, NC = 4, 8, 2
N = NX * NY * NC
NZ = 8
BLK = 512
HALF = 256
QUART = 128
PIECE = HALF // NY
ROWS = BLK // N
SLOTS = 8
ENTRIES = 2 * 2 * 512 * 4096

BF = jnp.bfloat16
F32 = jnp.float32
MESH = pl.DeviceIdType.MESH


def dev(y, x, c):
    return (lax.rem(y + NY, NY) * NX + lax.rem(x + NX, NX)) * NC + c


def owner_of(b):
    return (2 * b * NX + b) * NC


def mm(a, b):
    return jnp.dot(a, b, preferred_element_type=F32)


def mm_nt(a, b):
    return lax.dot_general(a, b, (((1,), (1,)), ((), ())), preferred_element_type=F32)


def mm_tn(a, b):
    return lax.dot_general(a, b, (((0,), (0,)), ((), ())), preferred_element_type=F32)


def kernel(
    table, g_hbm, f_hbm, v_hbm, p_hbm, out, nf_out,
    fac, inv, prb, send, recv,
    h, hr, xb, sbuf, yr, pb, sb, sall, zall, gbuf,
    lm, rm, km, hm, vm, ql, qr, wm, res, nf, nfr,
    load_sem, own_sem, d2d_s, d2d_r, x_s, x_r, fac_s, fac_r,
    y_s, y_r, g_s, g_r, s_s, s_r, z_s, z_r, ret_s, res_r, nf_r,
):
    i = lax.axis_index("dp")
    z = lax.axis_index("mp")
    c = lax.rem(i, NC)
    x = lax.rem(i // NC, NX)
    y = i // (NC * NX)
    is_owner = (c == 0) & (y == 2 * x)

    def remote(src, dst, ssem, rsem, d, zz=None):
        return pltpu.make_async_remote_copy(
            src_ref=src, dst_ref=dst, send_sem=ssem, recv_sem=rsem,
            device_id=(d, z if zz is None else zz), device_id_type=MESH,
        )

    def blk(o):
        return lax.rem(x + o, NX)

    loads = [
        pltpu.make_async_copy(f_hbm, fac, load_sem.at[0]),
        pltpu.make_async_copy(v_hbm, inv, load_sem.at[1]),
        pltpu.make_async_copy(p_hbm, prb, load_sem.at[2]),
    ]
    for cp in loads:
        cp.start()
    own = {}
    keep = pl.multiple_of(HALF * c, HALF)
    give = pl.multiple_of(HALF * (1 - c), HALF)
    for o in (2, 1, 3, 0):
        own[o] = pltpu.make_async_copy(g_hbm.at[blk(o), pl.ds(keep, HALF)], h.at[blk(o)], own_sem.at[o])
        own[o].start()

    bar = pltpu.get_barrier_semaphore()
    sib = dev(y, x, 1 - c)
    right, left = dev(y, x + 1, c), dev(y, x - 1, c)
    for d in [sib, right, left] + [dev(y + k, x, c) for k in range(1, NY)]:
        pl.semaphore_signal(bar, inc=1, device_id=(d, z), device_id_type=MESH)

    @pl.when(is_owner)
    def _():
        def tell(k, _):
            pl.semaphore_signal(bar, inc=1, device_id=(lax.rem(i + k, N), z), device_id_type=MESH)
            return 0

        lax.fori_loop(1, N, tell, 0)

        def tell_z(k, _):
            pl.semaphore_signal(bar, inc=1, device_id=(i, lax.rem(z + k, NZ)), device_id_type=MESH)
            return 0

        lax.fori_loop(1, NZ, tell_z, 0)
        pl.semaphore_wait(bar, 10 + 3 + NZ - 1)

    @pl.when(jnp.logical_not(is_owner))
    def _():
        pl.semaphore_wait(bar, 10 + 4)

    d2d = {}
    for o in (2, 1, 3, 0):
        d2d[o] = remote(g_hbm.at[blk(o), pl.ds(give, HALF)], hr.at[blk(o)], d2d_s.at[o], d2d_r.at[o], sib)
        d2d[o].start()

    for cp in loads:
        cp.wait()
    for b in range(NX):
        j = table[0, b]
        send[b, :, 0:1024] = fac[j]
        send[b, :, 1024:2048] = inv[j]
        send[b, :, 2048:2560] = prb[j]
    for b in range(NX):
        ow = owner_of(b)

        @pl.when(i != ow)
        def _():
            remote(send.at[b], recv.at[i], fac_s.at[b], fac_r, ow).start()

        @pl.when(i == ow)
        def _():
            pltpu.make_async_copy(send.at[b], recv.at[i], fac_r).start()

    def merge(o):
        own[o].wait()
        d2d[o].wait()
        h[blk(o)] = (h[blk(o)].astype(F32) + hr[blk(o)].astype(F32)).astype(BF)

    top, bot = pl.ds(0, QUART), pl.ds(QUART, QUART)

    def xsend(k, b, part, d):
        cp = remote(h.at[b, part], xb.at[k], x_s.at[k], x_r.at[k], d)
        cp.start()
        return cp

    merge(2)
    o_r = xsend(0, blk(2), top, right)
    o_l = xsend(1, blk(2), bot, left)
    merge(1)
    a_r = xsend(2, blk(1), bot, right)
    merge(3)
    a_l = xsend(3, blk(3), top, left)
    merge(0)
    o_r.wait_recv()
    h[blk(1), top] = (h[blk(1), top].astype(F32) + xb[0].astype(F32)).astype(BF)
    c_r = xsend(4, blk(1), top, right)
    o_l.wait_recv()
    h[blk(3), bot] = (h[blk(3), bot].astype(F32) + xb[1].astype(F32)).astype(BF)
    c_l = xsend(5, blk(3), bot, left)
    for cp in (a_r, a_l, c_r, c_l):
        cp.wait_recv()
    sbuf[top] = (h[x, top].astype(F32) + xb[3].astype(F32) + xb[4].astype(F32)).astype(BF)
    sbuf[bot] = (h[x, bot].astype(F32) + xb[2].astype(F32) + xb[5].astype(F32)).astype(BF)

    for k in (1, 7, 2, 6, 3, 5, 4):
        yy = lax.rem(y + k, NY)
        remote(sbuf.at[pl.ds(pl.multiple_of(PIECE * yy, PIECE), PIECE)], yr.at[y], y_s, y_r, dev(y + k, x, c)).start()
    yr[y] = sbuf[pl.ds(pl.multiple_of(PIECE * y, PIECE), PIECE)]
    for cp in (o_r, o_l, a_r, a_l, c_r, c_l):
        cp.wait_send()
    seven = yr.at[pl.ds(0, NY - 1)]
    pltpu.make_async_copy(seven, seven, y_r).wait()
    acc = yr[0].astype(F32)
    for k in range(1, NY):
        acc = acc + yr[k].astype(F32)
    pb[...] = acc.astype(BF)
    sq = jnp.sum(acc * acc, axis=0, keepdims=True)
    sb[...] = sq[:, 0:128] + sq[:, 128:256] + sq[:, 256:384] + sq[:, 384:512]

    mine = pl.ds(pl.multiple_of(HALF * c + PIECE * y, PIECE), PIECE)
    goal = dev(2 * x, x, 0)

    @pl.when(jnp.logical_not(is_owner))
    def _():
        remote(pb, gbuf.at[mine], g_s, g_r, goal).start()

    @pl.when(is_owner)
    def _():
        pltpu.make_async_copy(pb, gbuf.at[mine], g_r).start()

    for b in range(NX):
        ow = owner_of(b)

        @pl.when(i != ow)
        def _():
            remote(sb, sall.at[i], s_s.at[b], s_r, ow).start()

        @pl.when(i == ow)
        def _():
            pltpu.make_async_copy(sb, sall.at[i], s_r).start()

    @pl.when(is_owner)
    def _():
        pltpu.make_async_copy(recv, recv, fac_r).wait()

        def unpack(dst, lo):
            dst[...] = recv[:, :, lo : lo + BLK].astype(F32).reshape(BLK, BLK).astype(BF)

        unpack(lm, 0)
        unpack(rm, 512)
        unpack(km, 1024)
        unpack(hm, 1536)
        unpack(vm, 2048)
        wm[...] = mm_tn(km[...], vm[...]).astype(BF)
        wm[...] = mm(wm[...], hm[...]).astype(BF)
        ql[...] = mm_nt(wm[...], wm[...])
        qr[...] = mm_tn(wm[...], wm[...])

        pltpu.make_async_copy(sall, sall, s_r).wait()
        zall[z] = jnp.sum(sall[...], axis=0)

        def tell_z(k, _):
            remote(zall.at[z], zall.at[z], z_s, z_r, i, lax.rem(z + k, NZ)).start()
            return 0

        lax.fori_loop(1, NZ, tell_z, 0)
        pltpu.make_async_copy(gbuf, gbuf, g_r).wait()
        others = zall.at[pl.ds(0, NZ - 1)]
        pltpu.make_async_copy(others, others, z_r).wait()
        squares = jnp.sum(zall[...])
        clip = jnp.minimum(1.0, CLIP_RMS * math.sqrt(ENTRIES) * lax.rsqrt(jnp.full((1, 1), squares + EPS_NORM, F32)))
        gbuf[...] = (gbuf[...].astype(F32) * clip).astype(BF)
        vm[...] = mm(lm[...], gbuf[...]).astype(BF)
        wm[...] = mm_nt(vm[...], rm[...]).astype(BF)
        row = lax.broadcasted_iota(jnp.int32, (BLK, BLK), 0)
        col = lax.broadcasted_iota(jnp.int32, (BLK, BLK), 1)

        def step(factor, first, second):
            bound = jnp.max(jnp.abs(first + second)) + EPS_NORM
            change = jnp.where(row <= col, first - second, 0.0).astype(BF)
            moved = mm(change, factor)
            rate = LEARN_RATE / jnp.full((1, 1), bound, F32)
            return (factor.astype(F32) - rate * moved).astype(BF)

        km[...] = step(lm[...], mm_nt(wm[...], wm[...]), ql[...])
        hm[...] = step(rm[...], mm_tn(wm[...], wm[...]), qr[...])
        nf[:, :, 0:512] = km[...].astype(F32).reshape(N, ROWS, BLK).astype(BF)
        nf[:, :, 512:1024] = hm[...].astype(F32).reshape(N, ROWS, BLK).astype(BF)

        def back(k):
            j = (k + 1) // 2
            return lax.rem(jnp.where(lax.rem(k, 2) == 1, i + j, i + N - j), N)

        def back_nf(k, _):
            d = back(k)
            remote(nf.at[d], nfr.at[x], ret_s.at[0], nf_r.at[x], d).start()
            return 0

        lax.fori_loop(1, N, back_nf, 0)
        pltpu.make_async_copy(nf.at[i], nfr.at[x], nf_r.at[x]).start()
        vm[...] = mm_tn(km[...], km[...]).astype(BF)
        wm[...] = mm_tn(hm[...], hm[...]).astype(BF)
        vm[...] = mm(vm[...], gbuf[...]).astype(BF)
        res[...] = mm(vm[...], wm[...]).reshape(N, ROWS, BLK).astype(BF)

        def back_res(k, _):
            d = back(k)
            remote(res.at[d], out.at[x], ret_s.at[1], res_r.at[x], d).start()
            return 0

        lax.fori_loop(1, N, back_res, 0)
        pltpu.make_async_copy(res.at[i], out.at[x], res_r.at[x]).start()

    for b in range(NX):
        pltpu.make_async_copy(nfr.at[b], nfr.at[b], nf_r.at[b]).wait()
    for j in range(SLOTS):
        which = jnp.int32(0)
        hit = jnp.int32(0)
        for b in range(NX):
            same = table[0, b] == j
            which = jnp.where(same, b, which)
            hit = jnp.where(same, 1, hit)
        nf_out[j] = jnp.where(hit == 1, nfr[which].astype(F32), fac[j].astype(F32)).astype(BF)
    for b in range(NX):
        pltpu.make_async_copy(out.at[b], out.at[b], res_r.at[b]).wait()

    pltpu.make_async_copy(seven, seven, y_s).wait()
    for b in range(NX):
        ow = owner_of(b)

        @pl.when(i != ow)
        def _():
            pltpu.make_async_copy(send.at[b], send.at[b], fac_s.at[b]).wait()
            pltpu.make_async_copy(sb, sb, s_s.at[b]).wait()

    @pl.when(jnp.logical_not(is_owner))
    def _():
        pltpu.make_async_copy(pb, pb, g_s).wait()

    @pl.when(is_owner)
    def _():
        others = zall.at[pl.ds(0, NZ - 1)]
        pltpu.make_async_copy(others, others, z_s).wait()
        some = nf.at[pl.ds(0, N - 1)]
        pltpu.make_async_copy(some, some, ret_s.at[0]).wait()
        some = res.at[pl.ds(0, N - 1)]
        pltpu.make_async_copy(some, some, ret_s.at[1]).wait()


def body(partial_grads, factors, inverse_factors, probes, slot_table):
    grads = partial_grads.reshape(4, BLK, BLK)
    anywhere = pl.BlockSpec(memory_space=pl.ANY)
    vmem = pl.BlockSpec(memory_space=pltpu.VMEM)
    dma = pltpu.SemaphoreType.DMA
    V = pltpu.VMEM
    scratch = [
        V((SLOTS, ROWS, 1024), BF), V((SLOTS, ROWS, 1024), BF), V((SLOTS, ROWS, 512), BF),
        V((4, ROWS, 2560), BF), V((N, ROWS, 2560), BF),
        V((4, HALF, BLK), BF), V((4, HALF, BLK), BF), V((6, QUART, BLK), BF), V((HALF, BLK), BF),
        V((NY, PIECE, BLK), BF), V((PIECE, BLK), BF), V((1, 128), F32), V((N, 1, 128), F32),
        V((NZ, 1, 128), F32), V((BLK, BLK), BF),
        V((BLK, BLK), BF), V((BLK, BLK), BF), V((BLK, BLK), BF), V((BLK, BLK), BF), V((BLK, BLK), BF),
        V((BLK, BLK), F32), V((BLK, BLK), F32), V((BLK, BLK), BF),
        V((N, ROWS, BLK), BF), V((N, ROWS, 1024), BF), V((4, ROWS, 1024), BF),
        dma((3,)), dma((4,)), dma((4,)), dma((4,)), dma((6,)), dma((6,)), dma((4,)), dma,
        dma, dma, dma, dma, dma((4,)), dma, dma, dma, dma((2,)), dma((4,)), dma((4,)),
    ]
    out, nf = pl.pallas_call(
        kernel,
        out_shape=(
            jax.ShapeDtypeStruct((4, ROWS, BLK), BF),
            jax.ShapeDtypeStruct((SLOTS, ROWS, 1024), BF),
        ),
        in_specs=[pl.BlockSpec(memory_space=pltpu.SMEM)] + [anywhere] * 4,
        out_specs=(vmem, vmem),
        scratch_shapes=scratch,
        compiler_params=pltpu.CompilerParams(
            collective_id=1, has_side_effects=True, vmem_limit_bytes=62 * 1024 * 1024
        ),
    )(slot_table, grads, factors[0], inverse_factors[0], probes[0])
    return (out.reshape(2, 2, ROWS, BLK), nf[None])


def solution(mesh):
    return jax.shard_map(
        body,
        mesh=mesh,
        in_specs=(
            P("dp", None, None, None, "mp"),
            P("mp", None, "dp", None),
            P("mp", None, "dp", None),
            P("mp", None, "dp", None),
            P("mp", None),
        ),
        out_specs=(P(None, None, "dp", "mp"), P("mp", None, "dp", None)),
        check_vma=False,
    )
```

```python
import functools
import math

import jax
import jax.numpy as jnp
from jax import lax
from jax.experimental import pallas as pl
from jax.experimental.pallas import tpu as pltpu
from jax.sharding import PartitionSpec as P

CLIP_RMS = 0.3
LEARN_RATE = 0.1
EPS_NORM = 1e-06

NX, NY, NC = 4, 8, 2
N = NX * NY * NC
NZ = 8
BLK = 512
HALF = 256
QUART = 128
PIECE = HALF // NY
ROWS = BLK // N
SLOTS = 8
ENTRIES = 2 * 2 * 512 * 4096

BF = jnp.bfloat16
F32 = jnp.float32
MESH = pl.DeviceIdType.MESH


def dev(y, x, c):
    return (lax.rem(y + NY, NY) * NX + lax.rem(x + NX, NX)) * NC + c


def width(q):
    return BLK - 128 * q


def owner_of(b):
    return (2 * b * NX + b) * NC


def mm(a, b):
    return jnp.dot(a, b, preferred_element_type=F32)


def mm_nt(a, b):
    return lax.dot_general(a, b, (((1,), (1,)), ((), ())), preferred_element_type=F32)


def mm_tn(a, b):
    return lax.dot_general(a, b, (((0,), (0,)), ((), ())), preferred_element_type=F32)


def kernel(
    t_hbm, g_hbm, f_hbm, v_hbm, p_hbm, out, nfr,
    table, fac, inv, prb, send, relay, recv,
    h, hr, xb, sbuf, yr, pb, sb, sall, zall, gbuf,
    lm, rm, km, hm, vm, ql, qr, wm, res, nf,
    load_sem, own_sem, d2d_s, d2d_r, x_s, x_r, rel_s, rel_r, fac_s, fac_r,
    y_s, y_r, g_s, g_r, s_s, s_r, z_s, z_r, nf_s, res_s, res_r, nf_r,
):
    i = lax.axis_index("dp")
    z = lax.axis_index("mp")
    c = lax.rem(i, NC)
    x = lax.rem(i // NC, NX)
    y = i // (NC * NX)
    is_owner = (c == 0) & (y == 2 * x)
    band = y // 2

    def by_band(fn):
        for q in range(4):
            pl.when(band == q)(functools.partial(fn, q))

    def remote(src, dst, ssem, rsem, d, zz=None):
        return pltpu.make_async_remote_copy(
            src_ref=src, dst_ref=dst, send_sem=ssem, recv_sem=rsem,
            device_id=(d, z if zz is None else zz), device_id_type=MESH,
        )

    def blk(o):
        return lax.rem(x + o, NX)

    loads = [
        pltpu.make_async_copy(t_hbm, table, load_sem.at[3]),
        pltpu.make_async_copy(f_hbm, fac, load_sem.at[0]),
        pltpu.make_async_copy(v_hbm, inv, load_sem.at[1]),
        pltpu.make_async_copy(p_hbm, prb, load_sem.at[2]),
    ]
    for cp in loads:
        cp.start()
    own = {}
    keep = pl.multiple_of(HALF * c, HALF)
    give = pl.multiple_of(HALF * (1 - c), HALF)
    for o in (2, 1, 3, 0):
        own[o] = pltpu.make_async_copy(g_hbm.at[blk(o), pl.ds(keep, HALF)], h.at[blk(o)], own_sem.at[o])
        own[o].start()

    bar = pltpu.get_barrier_semaphore()
    sib = dev(y, x, 1 - c)
    right, left = dev(y, x + 1, c), dev(y, x - 1, c)
    for d in [sib, right, left, dev(y, x + 2, c)] + [dev(y + k, x, c) for k in range(1, NY)]:
        pl.semaphore_signal(bar, inc=1, device_id=(d, z), device_id_type=MESH)

    @pl.when(is_owner)
    def _():
        for k in range(1, NZ):
            pl.semaphore_signal(bar, inc=1, device_id=(i, lax.rem(z + k, NZ)), device_id_type=MESH)
        pl.semaphore_wait(bar, 11 + NZ - 1)

    @pl.when(jnp.logical_not(is_owner))
    def _():
        pl.semaphore_wait(bar, 11)

    d2d = {}
    for o in (2, 1, 3, 0):
        d2d[o] = remote(g_hbm.at[blk(o), pl.ds(give, HALF)], hr.at[blk(o)], d2d_s.at[o], d2d_r.at[o], sib)
        d2d[o].start()

    for cp in loads:
        cp.wait()

    def pack(q):
        w = width(q)
        total = 4 * w + BLK
        for b in range(NX):
            j = table[0, b]
            for k, src in ((0, fac), (1, fac), (2, inv), (3, inv)):
                lo = BLK * (k % 2)
                send[b, :, k * w : (k + 1) * w] = src[j, :, lo + BLK - w : lo + BLK]
            send[b, :, 4 * w : total] = prb[j]
        for k in (1, 3, 2):
            to = blk(k)
            remote(
                send.at[to, :, pl.ds(0, total)], relay.at[x, :, pl.ds(0, total)],
                rel_s, rel_r, dev(y, x + k, c),
            ).start()
        relay[x, :, 0:total] = send[x, :, 0:total]

    by_band(pack)

    def forward(q):
        total = 4 * width(q) + BLK
        three = relay.at[pl.ds(0, 3), :, pl.ds(0, total)]
        pltpu.make_async_copy(three, three, rel_r).wait()
        src = relay.at[:, :, pl.ds(0, total)]
        dst = recv.at[y, :, c, :, pl.ds(0, total)]

        @pl.when(jnp.logical_not(is_owner))
        def _():
            remote(src, dst, fac_s, fac_r.at[q], dev(2 * x, x, 0)).start()

        @pl.when(is_owner)
        def _():
            pltpu.make_async_copy(src, dst, fac_r.at[q]).start()

    def merge(o):
        own[o].wait()
        d2d[o].wait()
        h[blk(o)] = (h[blk(o)].astype(F32) + hr[blk(o)].astype(F32)).astype(BF)

    top, bot = pl.ds(0, QUART), pl.ds(QUART, QUART)

    def xsend(k, b, part, d):
        cp = remote(h.at[b, part], xb.at[k], x_s.at[k], x_r.at[k], d)
        cp.start()
        return cp

    merge(2)
    o_r = xsend(0, blk(2), top, right)
    o_l = xsend(1, blk(2), bot, left)
    merge(1)
    a_r = xsend(2, blk(1), bot, right)
    merge(3)
    a_l = xsend(3, blk(3), top, left)
    by_band(forward)
    merge(0)
    o_r.wait_recv()
    h[blk(1), top] = (h[blk(1), top].astype(F32) + xb[0].astype(F32)).astype(BF)
    c_r = xsend(4, blk(1), top, right)
    o_l.wait_recv()
    h[blk(3), bot] = (h[blk(3), bot].astype(F32) + xb[1].astype(F32)).astype(BF)
    c_l = xsend(5, blk(3), bot, left)
    for cp in (a_r, a_l, c_r, c_l):
        cp.wait_recv()
    sbuf[top] = (h[x, top].astype(F32) + xb[3].astype(F32) + xb[4].astype(F32)).astype(BF)
    sbuf[bot] = (h[x, bot].astype(F32) + xb[2].astype(F32) + xb[5].astype(F32)).astype(BF)

    for k in (1, 7, 2, 6, 3, 5, 4):
        yy = lax.rem(y + k, NY)
        remote(sbuf.at[pl.ds(pl.multiple_of(PIECE * yy, PIECE), PIECE)], yr.at[y], y_s, y_r, dev(y + k, x, c)).start()
    yr[y] = sbuf[pl.ds(pl.multiple_of(PIECE * y, PIECE), PIECE)]
    for cp in (o_r, o_l, a_r, a_l, c_r, c_l):
        cp.wait_send()
    seven = yr.at[pl.ds(0, NY - 1)]
    pltpu.make_async_copy(seven, seven, y_r).wait()
    acc = yr[0].astype(F32)
    for k in range(1, NY):
        acc = acc + yr[k].astype(F32)
    pb[...] = acc.astype(BF)
    sq = jnp.sum(acc * acc, axis=0, keepdims=True)
    sb[...] = sq[:, 0:128] + sq[:, 128:256] + sq[:, 256:384] + sq[:, 384:512]

    mine = pl.ds(pl.multiple_of(HALF * c + PIECE * y, PIECE), PIECE)
    goal = dev(2 * x, x, 0)

    @pl.when(jnp.logical_not(is_owner))
    def _():
        remote(pb, gbuf.at[mine], g_s, g_r, goal).start()

    @pl.when(is_owner)
    def _():
        pltpu.make_async_copy(pb, gbuf.at[mine], g_r).start()

    for b in range(NX):
        ow = owner_of(b)

        @pl.when(i != ow)
        def _():
            remote(sb, sall.at[i], s_s.at[b], s_r, ow).start()

        @pl.when(i == ow)
        def _():
            pltpu.make_async_copy(sb, sall.at[i], s_r).start()

    @pl.when(is_owner)
    def _():
        for m in (lm, rm, km, hm):
            for q in range(1, 4):
                m[128 * q : 128 * (q + 1), 0 : 128 * q] = jnp.zeros((128, 128 * q), BF)
        for q in range(4):
            w = width(q)
            got = recv.at[pl.ds(2 * q, 2), :, :, :, pl.ds(0, 4 * w + BLK)]
            pltpu.make_async_copy(got, got, fac_r.at[q]).wait()
        for q in range(4):
            w = width(q)
            rows = slice(128 * q, 128 * (q + 1))
            for k, m in enumerate((lm, rm, km, hm)):
                part = recv[2 * q : 2 * q + 2, :, :, :, k * w : (k + 1) * w]
                m[rows, BLK - w : BLK] = part.astype(F32).reshape(128, w).astype(BF)
            part = recv[2 * q : 2 * q + 2, :, :, :, 4 * w : 4 * w + BLK]
            vm[rows] = part.astype(F32).reshape(128, BLK).astype(BF)
        wm[...] = mm_tn(km[...], vm[...]).astype(BF)
        wm[...] = mm(wm[...], hm[...]).astype(BF)
        ql[...] = mm_nt(wm[...], wm[...])
        qr[...] = mm_tn(wm[...], wm[...])

        pltpu.make_async_copy(sall, sall, s_r).wait()
        zall[z] = jnp.sum(sall[...], axis=0)

        def tell_z(k, _):
            remote(zall.at[z], zall.at[z], z_s, z_r, i, lax.rem(z + k, NZ)).start()
            return 0

        lax.fori_loop(1, NZ, tell_z, 0)
        pltpu.make_async_copy(gbuf, gbuf, g_r).wait()
        others = zall.at[pl.ds(0, NZ - 1)]
        pltpu.make_async_copy(others, others, z_r).wait()
        squares = jnp.sum(zall[...])
        clip = jnp.minimum(1.0, CLIP_RMS * math.sqrt(ENTRIES) * lax.rsqrt(jnp.full((1, 1), squares + EPS_NORM, F32)))
        gbuf[...] = (gbuf[...].astype(F32) * clip).astype(BF)
        vm[...] = mm(lm[...], gbuf[...]).astype(BF)
        wm[...] = mm_nt(vm[...], rm[...]).astype(BF)
        row = lax.broadcasted_iota(jnp.int32, (BLK, BLK), 0)
        col = lax.broadcasted_iota(jnp.int32, (BLK, BLK), 1)

        def step(factor, first, second):
            bound = jnp.max(jnp.abs(first + second)) + EPS_NORM
            change = jnp.where(row <= col, first - second, 0.0).astype(BF)
            moved = mm(change, factor)
            rate = LEARN_RATE / jnp.full((1, 1), bound, F32)
            return (factor.astype(F32) - rate * moved).astype(BF)

        km[...] = step(lm[...], mm_nt(wm[...], wm[...]), ql[...])
        hm[...] = step(rm[...], mm_tn(wm[...], wm[...]), qr[...])
        for q in range(4):
            w = width(q)
            for k, m in enumerate((km, hm)):
                part = m[128 * q : 128 * (q + 1), BLK - w : BLK]
                nf[16 * q : 16 * (q + 1), :, k * w : (k + 1) * w] = part.astype(F32).reshape(16, ROWS, w).astype(BF)

        def back(src, dst, sems, rsem, t, q, w):
            d = 16 * q + t
            s_ref = src.at[d, :, pl.ds(0, w)]
            d_ref = dst.at[x, :, pl.ds(0, w)]

            @pl.when(d != i)
            def _():
                remote(s_ref, d_ref, sems.at[q], rsem.at[x], d).start()

            @pl.when(d == i)
            def _():
                pltpu.make_async_copy(s_ref, d_ref, rsem.at[x]).start()

        def back_nf(t, _):
            for q in range(4):
                back(nf, nfr, nf_s, nf_r, t, q, 2 * width(q))
            return 0

        lax.fori_loop(0, 16, back_nf, 0)
        vm[...] = mm_tn(km[...], km[...]).astype(BF)
        wm[...] = mm_tn(hm[...], hm[...]).astype(BF)
        vm[...] = mm(vm[...], gbuf[...]).astype(BF)
        res[...] = mm(vm[...], wm[...]).reshape(N, ROWS, BLK).astype(BF)

        def back_res(t, _):
            for q in range(4):
                back(res, out, res_s, res_r, t, q, BLK)
            return 0

        lax.fori_loop(0, 16, back_res, 0)

    def landed(q):
        for b in range(NX):
            part = nfr.at[b, :, pl.ds(0, 2 * width(q))]
            pltpu.make_async_copy(part, part, nf_r.at[b]).wait()

    by_band(landed)
    for b in range(NX):
        pltpu.make_async_copy(out.at[b], out.at[b], res_r.at[b]).wait()

    pltpu.make_async_copy(seven, seven, y_s).wait()

    def sent(q):
        total = 4 * width(q) + BLK
        three = relay.at[pl.ds(0, 3), :, pl.ds(0, total)]
        pltpu.make_async_copy(three, three, rel_s).wait()

        @pl.when(jnp.logical_not(is_owner))
        def _():
            four = relay.at[:, :, pl.ds(0, total)]
            pltpu.make_async_copy(four, four, fac_s).wait()

    by_band(sent)
    for b in range(NX):

        @pl.when(i != owner_of(b))
        def _():
            pltpu.make_async_copy(sb, sb, s_s.at[b]).wait()

    @pl.when(jnp.logical_not(is_owner))
    def _():
        pltpu.make_async_copy(pb, pb, g_s).wait()

    @pl.when(is_owner)
    def _():
        others = zall.at[pl.ds(0, NZ - 1)]
        pltpu.make_async_copy(others, others, z_s).wait()

        def gone(src, sem, count, w):
            some = src.at[pl.ds(0, count), :, pl.ds(0, w)]
            pltpu.make_async_copy(some, some, sem).wait()

        for q in range(4):

            @pl.when(band == q)
            def _():
                gone(nf, nf_s.at[q], 15, 2 * width(q))
                gone(res, res_s.at[q], 15, BLK)

            @pl.when(band != q)
            def _():
                gone(nf, nf_s.at[q], 16, 2 * width(q))
                gone(res, res_s.at[q], 16, BLK)


def assemble(table, fac, rows, fresh, out, nf):
    q = lax.axis_index("dp") // 16
    out[...] = rows[...]
    for j in range(SLOTS):
        which = jnp.int32(0)
        hit = jnp.int32(0)
        for b in range(NX):
            same = table[0, b] == j
            which = jnp.where(same, b, which)
            hit = jnp.where(same, 1, hit)
        for k in range(4):

            @pl.when(q == k)
            def _():
                w = width(k)
                for side in range(2):
                    lo = BLK * side
                    old = fac[j, :, lo + BLK - w : lo + BLK]
                    new = fresh[which, :, side * w : (side + 1) * w]
                    nf[j, :, lo + BLK - w : lo + BLK] = jnp.where(hit == 1, new.astype(F32), old.astype(F32)).astype(BF)
                    if k:
                        nf[j, :, lo : lo + BLK - w] = jnp.zeros((ROWS, BLK - w), BF)


def body(partial_grads, factors, inverse_factors, probes, slot_table):
    grads = partial_grads.reshape(4, BLK, BLK)
    anywhere = pl.BlockSpec(memory_space=pl.ANY)
    vmem = pl.BlockSpec(memory_space=pltpu.VMEM)
    dma = pltpu.SemaphoreType.DMA
    V = pltpu.VMEM
    scratch = [
        pltpu.SMEM((1, 4), jnp.int32),
        V((SLOTS, ROWS, 1024), BF), V((SLOTS, ROWS, 1024), BF), V((SLOTS, ROWS, 512), BF),
        V((4, ROWS, 2560), BF), V((4, ROWS, 2560), BF), V((NY, NX, NC, ROWS, 2560), BF),
        V((4, HALF, BLK), BF), V((4, HALF, BLK), BF), V((6, QUART, BLK), BF), V((HALF, BLK), BF),
        V((NY, PIECE, BLK), BF), V((PIECE, BLK), BF), V((1, 128), F32), V((N, 1, 128), F32),
        V((NZ, 1, 128), F32), V((BLK, BLK), BF),
        V((BLK, BLK), BF), V((BLK, BLK), BF), V((BLK, BLK), BF), V((BLK, BLK), BF), V((BLK, BLK), BF),
        V((BLK, BLK), F32), V((BLK, BLK), F32), V((BLK, BLK), BF),
        V((N, ROWS, BLK), BF), V((N, ROWS, 1024), BF),
        dma((4,)), dma((4,)), dma((4,)), dma((4,)), dma((6,)), dma((6,)), dma, dma, dma, dma((4,)),
        dma, dma, dma, dma, dma((4,)), dma, dma, dma, dma((4,)), dma((4,)), dma((4,)), dma((4,)),
    ]
    rows, fresh = pl.pallas_call(
        kernel,
        out_shape=(
            jax.ShapeDtypeStruct((4, ROWS, BLK), BF),
            jax.ShapeDtypeStruct((4, ROWS, 1024), BF),
        ),
        in_specs=[anywhere] * 5,
        out_specs=(anywhere, anywhere),
        scratch_shapes=scratch,
        compiler_params=pltpu.CompilerParams(
            collective_id=1, has_side_effects=True, vmem_limit_bytes=62 * 1024 * 1024
        ),
    )(slot_table, grads, factors[0], inverse_factors[0], probes[0])
    out, nf = pl.pallas_call(
        assemble,
        out_shape=(
            jax.ShapeDtypeStruct((4, ROWS, BLK), BF),
            jax.ShapeDtypeStruct((SLOTS, ROWS, 1024), BF),
        ),
        in_specs=[pl.BlockSpec(memory_space=pltpu.SMEM), vmem, vmem, vmem],
        out_specs=(vmem, vmem),
    )(slot_table, factors[0], rows, fresh)
    return (out.reshape(2, 2, ROWS, BLK), nf[None])


def solution(mesh):
    return jax.shard_map(
        body,
        mesh=mesh,
        in_specs=(
            P("dp", None, None, None, "mp"),
            P("mp", None, "dp", None),
            P("mp", None, "dp", None),
            P("mp", None, "dp", None),
            P("mp", None),
        ),
        out_specs=(P(None, None, "dp", "mp"), P("mp", None, "dp", None)),
        check_vma=False,
    )
```

```python
import functools
import math

import jax
import jax.numpy as jnp
from jax import lax
from jax.experimental import pallas as pl
from jax.experimental.pallas import tpu as pltpu
from jax.sharding import PartitionSpec as P

CLIP_RMS = 0.3
LEARN_RATE = 0.1
EPS_NORM = 1e-06

NX, NY, NC = 4, 8, 2
N = NX * NY * NC
NZ = 8
BLK = 512
HALF = 256
SETS = 2
SET = HALF // SETS
PART = SET // 2
PIECE = SET // NY
ROWS = BLK // N
SLOTS = 8
ENTRIES = 2 * 2 * 512 * 4096

BF = jnp.bfloat16
F32 = jnp.float32
MESH = pl.DeviceIdType.MESH


def dev(y, x, c):
    return (lax.rem(y + NY, NY) * NX + lax.rem(x + NX, NX)) * NC + c


def width(q):
    return BLK - 128 * q


def owner_of(b, k):
    return ((2 + 4 * k) * NX + b) * NC


def mm(a, b):
    return jnp.dot(a, b, preferred_element_type=F32)


def mm_nt(a, b):
    return lax.dot_general(a, b, (((1,), (1,)), ((), ())), preferred_element_type=F32)


def mm_tn(a, b):
    return lax.dot_general(a, b, (((0,), (0,)), ((), ())), preferred_element_type=F32)


def kernel(
    t_hbm, g_hbm, f_hbm, v_hbm, p_hbm, out, nfr,
    table, fac, inv, prb, send, relay, recv,
    h, hr, xb, sbuf, yr, y4, pb, sb, sall, zall, gbuf,
    lm, rm, km, hm, vm, ql, qr, pn, mid, wm, res, nf,
    load_sem, own_sem, d2d_s, d2d_r, x_s, x_r, rel_s, rel_r, fac_s, fac_r,
    y_s, y_r, y4_r, g_s, g_r, s_s, s_r, z_s, z_r, nf_s, res_s, res_r, nf_r,
):
    i = lax.axis_index("dp")
    z = lax.axis_index("mp")
    c = lax.rem(i, NC)
    x = lax.rem(i // NC, NX)
    y = i // (NC * NX)
    is_owner = (c == 0) & (lax.rem(y, 4) == 2)
    band = y // 2

    def to_owners(src, dst, ssem, rsem):
        for k in range(2):
            goal = dev(2 + 4 * k, x, 0)

            @pl.when(i != goal)
            def _():
                remote(src, dst, ssem.at[k], rsem, goal).start()

            @pl.when(i == goal)
            def _():
                pltpu.make_async_copy(src, dst, rsem).start()

    def owners_sent(src, ssem):
        for k in range(2):

            @pl.when(i != dev(2 + 4 * k, x, 0))
            def _():
                pltpu.make_async_copy(src, src, ssem.at[k]).wait()

    def by_band(fn):
        for q in range(4):
            pl.when(band == q)(functools.partial(fn, q))

    def remote(src, dst, ssem, rsem, d, zz=None):
        return pltpu.make_async_remote_copy(
            src_ref=src, dst_ref=dst, send_sem=ssem, recv_sem=rsem,
            device_id=(d, z if zz is None else zz), device_id_type=MESH,
        )

    def blk(o):
        return lax.rem(x + o, NX)

    loads = [
        pltpu.make_async_copy(t_hbm, table, load_sem.at[3]),
        pltpu.make_async_copy(f_hbm, fac, load_sem.at[0]),
        pltpu.make_async_copy(v_hbm, inv, load_sem.at[1]),
        pltpu.make_async_copy(p_hbm, prb, load_sem.at[2]),
    ]
    for cp in loads:
        cp.start()
    own = {}
    keep = pl.multiple_of(HALF * c, HALF)
    give = pl.multiple_of(HALF * (1 - c), HALF)
    order = ((2, 0), (2, 1), (1, 0), (3, 0), (1, 1), (3, 1), (0, 0), (0, 1))
    for o, s in order:
        own[o, s] = pltpu.make_async_copy(
            g_hbm.at[blk(o), pl.ds(keep + SET * s, SET)], h.at[blk(o), pl.ds(SET * s, SET)], own_sem.at[2 * o + s]
        )
        own[o, s].start()

    bar = pltpu.get_barrier_semaphore()
    sib = dev(y, x, 1 - c)
    right, left = dev(y, x + 1, c), dev(y, x - 1, c)
    for d in [sib, right, left, dev(y, x + 2, c)] + [dev(y + k, x, c) for k in range(1, NY)]:
        pl.semaphore_signal(bar, inc=1, device_id=(d, z), device_id_type=MESH)

    @pl.when(is_owner)
    def _():
        for k in range(1, NZ):
            pl.semaphore_signal(bar, inc=1, device_id=(i, lax.rem(z + k, NZ)), device_id_type=MESH)
        pl.semaphore_wait(bar, 11 + NZ - 1)

    @pl.when(jnp.logical_not(is_owner))
    def _():
        pl.semaphore_wait(bar, 11)

    d2d = {}
    for o, s in order:
        d2d[o, s] = remote(
            g_hbm.at[blk(o), pl.ds(give + SET * s, SET)], hr.at[blk(o), pl.ds(SET * s, SET)],
            d2d_s.at[2 * o + s], d2d_r.at[2 * o + s], sib,
        )
        d2d[o, s].start()

    for cp in loads:
        cp.wait()

    def pack(q):
        w = width(q)
        total = 4 * w + BLK
        for b in range(NX):
            j = table[0, b]
            for k, src in ((0, fac), (1, fac), (2, inv), (3, inv)):
                lo = BLK * (k % 2)
                send[b, :, k * w : (k + 1) * w] = src[j, :, lo + BLK - w : lo + BLK]
            send[b, :, 4 * w : total] = prb[j]
        for k in (1, 3, 2):
            to = blk(k)
            remote(
                send.at[to, :, pl.ds(0, total)], relay.at[x, :, pl.ds(0, total)],
                rel_s, rel_r, dev(y, x + k, c),
            ).start()
        relay[x, :, 0:total] = send[x, :, 0:total]

    by_band(pack)

    def forward(q):
        total = 4 * width(q) + BLK
        three = relay.at[pl.ds(0, 3), :, pl.ds(0, total)]
        pltpu.make_async_copy(three, three, rel_r).wait()
        src = relay.at[:, :, pl.ds(0, total)]
        dst = recv.at[y, :, c, :, pl.ds(0, total)]

        to_owners(src, dst, fac_s, fac_r.at[q])

    def merge(o, s):
        own[o, s].wait()
        d2d[o, s].wait()
        part = pl.ds(SET * s, SET)
        h[blk(o), part] = (h[blk(o), part].astype(F32) + hr[blk(o), part].astype(F32)).astype(BF)

    def top(s):
        return pl.ds(SET * s, PART)

    def bot(s):
        return pl.ds(SET * s + PART, PART)

    xs = {}

    def xsend(k, s, b, part, d):
        n = 6 * s + k
        xs[k, s] = remote(h.at[b, part], xb.at[n], x_s.at[n], x_r.at[n], d)
        xs[k, s].start()

    def plus(k, s, b, part):
        xs[k, s].wait_recv()
        h[b, part] = (h[b, part].astype(F32) + xb[6 * s + k].astype(F32)).astype(BF)

    for s in range(SETS):
        merge(2, s)
        xsend(0, s, blk(2), top(s), right)
        xsend(1, s, blk(2), bot(s), left)
    merge(1, 0)
    xsend(2, 0, blk(1), bot(0), right)
    merge(3, 0)
    xsend(3, 0, blk(3), top(0), left)
    merge(1, 1)
    merge(3, 1)
    by_band(forward)
    for s in range(SETS):
        plus(0, s, blk(1), top(s))
        xsend(4, s, blk(1), top(s), right)
        plus(1, s, blk(3), bot(s))
        xsend(5, s, blk(3), bot(s), left)
        if s == 0:
            xsend(2, 1, blk(1), bot(1), right)
            xsend(3, 1, blk(3), top(1), left)
    merge(0, 0)
    merge(0, 1)

    def piece(s, k):
        return pl.ds(SET * s + pl.multiple_of(PIECE * lax.rem(y + k, NY), PIECE), PIECE)

    def ysend(s, slot, k):
        remote(sbuf.at[piece(s, k)], yr.at[s, slot], y_s.at[s], y_r.at[s], dev(y + k, x, c)).start()

    far = {}
    for s in range(SETS):
        for k in (2, 3, 4, 5):
            xs[k, s].wait_recv()
        n = 6 * s
        sbuf[top(s)] = (h[x, top(s)].astype(F32) + xb[n + 3].astype(F32) + xb[n + 4].astype(F32)).astype(BF)
        sbuf[bot(s)] = (h[x, bot(s)].astype(F32) + xb[n + 2].astype(F32) + xb[n + 5].astype(F32)).astype(BF)
        far[s] = remote(sbuf.at[piece(s, 4)], y4.at[s], y_s.at[s], y4_r.at[s], dev(y + 7, x, c))
        far[s].start()
        for slot, k in enumerate((3, 6, 2, 7, 1)):
            ysend(s, slot, k)

    for s in range(SETS):
        far[s].wait_recv()
        sbuf[piece(s, 5)] = (sbuf[piece(s, 5)].astype(F32) + y4[s].astype(F32)).astype(BF)
        ysend(s, 5, 5)
    for cp in xs.values():
        cp.wait_send()
    sq = jnp.zeros((1, BLK), F32)

    def ysum(s):
        pltpu.make_async_copy(yr.at[s], yr.at[s], y_r.at[s]).wait()
        acc = sbuf[piece(s, 0)].astype(F32)
        for k in range(NY - 2):
            acc = acc + yr[s, k].astype(F32)
        pb[s] = acc.astype(BF)
        return jnp.sum(acc * acc, axis=0, keepdims=True)

    def pieces(s):
        mine = pl.ds(pl.multiple_of(HALF * c + SET * s + PIECE * y, PIECE), PIECE)
        to_owners(pb.at[s], gbuf.at[mine], g_s.at[s], g_r)

    sq = ysum(0)
    pieces(0)
    sq = sq + ysum(1)
    sb[...] = sq[:, 0:128] + sq[:, 128:256] + sq[:, 256:384] + sq[:, 384:512]

    for b in range(NX):
        for k in range(2):
            ow = owner_of(b, k)

            @pl.when(i != ow)
            def _():
                remote(sb, sall.at[y, x, c], s_s.at[2 * b + k], s_r, ow).start()

            @pl.when(i == ow)
            def _():
                pltpu.make_async_copy(sb, sall.at[y, x, c], s_r).start()

    pieces(1)

    @pl.when(is_owner)
    def _():
        for m in (lm, rm, km, hm):
            for q in range(1, 4):
                m[128 * q : 128 * (q + 1), 0 : 128 * q] = jnp.zeros((128, 128 * q), BF)
        for q in range(4):
            w = width(q)
            got = recv.at[pl.ds(2 * q, 2), :, :, :, pl.ds(0, 4 * w + BLK)]
            pltpu.make_async_copy(got, got, fac_r.at[q]).wait()
        for q in range(4):
            w = width(q)
            rows = slice(128 * q, 128 * (q + 1))
            for k, m in enumerate((lm, rm, km, hm)):
                part = recv[2 * q : 2 * q + 2, :, :, :, k * w : (k + 1) * w]
                m[rows, BLK - w : BLK] = part.astype(F32).reshape(128, w).astype(BF)
            part = recv[2 * q : 2 * q + 2, :, :, :, 4 * w : 4 * w + BLK]
            vm[rows] = part.astype(F32).reshape(128, BLK).astype(BF)
        row = lax.broadcasted_iota(jnp.int32, (BLK, BLK), 0)
        col = lax.broadcasted_iota(jnp.int32, (BLK, BLK), 1)

        def full(v):
            return jnp.full((1, 1), v, F32)

        def upper(m):
            return jnp.where(row <= col, m, 0.0).astype(BF)

        def scaled(m):
            top_value = jnp.maximum(jnp.max(jnp.abs(m)), 1e-30)
            return (m * (1.0 / full(top_value))).astype(BF), top_value

        wm[...] = mm_tn(km[...], vm[...]).astype(BF)
        wm[...], q_top = scaled(mm(wm[...], hm[...]))
        for side, (m, gram) in enumerate(((lm, mm_nt), (rm, mm_tn))):
            value = gram(wm[...], wm[...])
            (ql, qr)[side][...] = value
            mid[side] = mm(upper(value), m[...])

        pltpu.make_async_copy(sall, sall, s_r).wait()
        zall[z] = jnp.sum(sall[...], axis=(0, 1, 2))
        local = jnp.sum(sall[:, x])

        def tell_z(k, _):
            remote(zall.at[z], zall.at[z], z_s, z_r, i, lax.rem(z + k, NZ)).start()
            return 0

        lax.fori_loop(1, NZ, tell_z, 0)
        limit = CLIP_RMS * math.sqrt(ENTRIES)

        def clip_of(squares):
            return jnp.minimum(1.0, limit * lax.rsqrt(full(squares + EPS_NORM)))

        pltpu.make_async_copy(gbuf, gbuf, g_r).wait()
        first_clip = clip_of(local)
        gbuf[...] = (gbuf[...].astype(F32) * first_clip).astype(BF)
        vm[...] = mm(lm[...], gbuf[...]).astype(BF)
        wm[...], p_top = scaled(mm_nt(vm[...], rm[...]))
        for side, (m, gram) in enumerate(((lm, mm_nt), (rm, mm_tn))):
            value = gram(wm[...], wm[...])
            pn[side] = value
            mid[2 + side] = mm(upper(value), m[...])
        others = zall.at[pl.ds(0, NZ - 1)]
        pltpu.make_async_copy(others, others, z_r).wait()
        ratio = clip_of(jnp.sum(zall[...])) / first_clip
        gbuf[...] = (gbuf[...].astype(F32) * ratio).astype(BF)
        p_scale = (ratio * p_top) * (ratio * p_top)
        q_scale = full(q_top) * full(q_top)
        for side, (m, q_ref, new) in enumerate(((lm, ql, km), (rm, qr, hm))):
            bound = jnp.max(jnp.abs(p_scale * pn[side] + q_scale * q_ref[...])) + EPS_NORM
            rate = LEARN_RATE / full(bound)
            moved = (rate * p_scale) * mid[2 + side] - (rate * q_scale) * mid[side]
            new[...] = (m[...].astype(F32) - moved).astype(BF)
        for q in range(4):
            w = width(q)
            for k, m in enumerate((km, hm)):
                part = m[128 * q : 128 * (q + 1), BLK - w : BLK]
                nf[16 * q : 16 * (q + 1), :, k * w : (k + 1) * w] = part.astype(F32).reshape(16, ROWS, w).astype(BF)

        def back(src, dst, sems, rsem, widths):
            def column(t, _):
                for yy in range(NY):
                    gap = lax.rem(yy + NY - y, NY)
                    odd = lax.rem(t, 2)
                    w = widths[yy // 2]
                    d = NX * NC * yy + t
                    s_ref = src.at[d, :, pl.ds(0, w)]
                    d_ref = dst.at[x, :, pl.ds(0, w)]
                    near = (gap <= 1) | (gap == 7) | ((gap == 2) & (odd == 0)) | ((gap == 6) & (odd == 1))

                    @pl.when(near & (d != i))
                    def _():
                        remote(s_ref, d_ref, sems.at[yy], rsem.at[x], d).start()

                    @pl.when(d == i)
                    def _():
                        pltpu.make_async_copy(s_ref, d_ref, rsem.at[x]).start()

                return 0

            lax.fori_loop(0, NX * NC, column, 0)

        nf_widths = [2 * width(q) for q in range(4)]
        res_widths = [BLK] * 4
        back(nf, nfr, nf_s, nf_r, nf_widths)
        vm[...] = mm_tn(km[...], km[...]).astype(BF)
        wm[...] = mm_tn(hm[...], hm[...]).astype(BF)
        vm[...] = mm(vm[...], gbuf[...]).astype(BF)
        res[...] = mm(vm[...], wm[...]).reshape(N, ROWS, BLK).astype(BF)

        back(res, out, res_s, res_r, res_widths)

    def landed(q):
        for b in range(NX):
            part = nfr.at[b, :, pl.ds(0, 2 * width(q))]
            pltpu.make_async_copy(part, part, nf_r.at[b]).wait()

    by_band(landed)
    for b in range(NX):
        pltpu.make_async_copy(out.at[b], out.at[b], res_r.at[b]).wait()

    seven = sbuf.at[pl.ds(0, 7 * PIECE)]
    for s in range(SETS):
        pltpu.make_async_copy(seven, seven, y_s.at[s]).wait()

    def sent(q):
        total = 4 * width(q) + BLK
        three = relay.at[pl.ds(0, 3), :, pl.ds(0, total)]
        pltpu.make_async_copy(three, three, rel_s).wait()

        owners_sent(relay.at[:, :, pl.ds(0, total)], fac_s)

    by_band(sent)
    for s in range(SETS):
        owners_sent(pb.at[s], g_s.at[s])
    for b in range(NX):
        for k in range(2):

            @pl.when(i != owner_of(b, k))
            def _():
                pltpu.make_async_copy(sb, sb, s_s.at[2 * b + k]).wait()

    @pl.when(is_owner)
    def _():
        others = zall.at[pl.ds(0, NZ - 1)]
        pltpu.make_async_copy(others, others, z_s).wait()

        nf_widths = [2 * width(q) for q in range(4)]

        def gone(src, sem, count, w):
            some = src.at[pl.ds(0, count), :, pl.ds(0, w)]
            pltpu.make_async_copy(some, some, sem).wait()

        for yy in range(NY):
            gap = lax.rem(yy + NY - y, NY)
            for count, here in ((7, gap == 0), (8, (gap == 1) | (gap == 7)), (4, (gap == 2) | (gap == 6))):

                @pl.when(here)
                def _():
                    gone(nf, nf_s.at[yy], count, nf_widths[yy // 2])
                    gone(res, res_s.at[yy], count, BLK)


def assemble(table, fac, rows, fresh, out, nf):
    q = lax.axis_index("dp") // 16
    out[...] = rows[...]
    for j in range(SLOTS):
        which = jnp.int32(0)
        hit = jnp.int32(0)
        for b in range(NX):
            same = table[0, b] == j
            which = jnp.where(same, b, which)
            hit = jnp.where(same, 1, hit)
        for k in range(4):

            @pl.when(q == k)
            def _():
                w = width(k)
                for side in range(2):
                    lo = BLK * side
                    old = fac[j, :, lo + BLK - w : lo + BLK]
                    new = fresh[which, :, side * w : (side + 1) * w]
                    nf[j, :, lo + BLK - w : lo + BLK] = jnp.where(hit == 1, new.astype(F32), old.astype(F32)).astype(BF)
                    if k:
                        nf[j, :, lo : lo + BLK - w] = jnp.zeros((ROWS, BLK - w), BF)


def body(partial_grads, factors, inverse_factors, probes, slot_table):
    grads = partial_grads.reshape(4, BLK, BLK)
    anywhere = pl.BlockSpec(memory_space=pl.ANY)
    vmem = pl.BlockSpec(memory_space=pltpu.VMEM)
    dma = pltpu.SemaphoreType.DMA
    V = pltpu.VMEM
    scratch = [
        pltpu.SMEM((1, 4), jnp.int32),
        V((SLOTS, ROWS, 1024), BF), V((SLOTS, ROWS, 1024), BF), V((SLOTS, ROWS, 512), BF),
        V((4, ROWS, 2560), BF), V((4, ROWS, 2560), BF), V((NY, NX, NC, ROWS, 2560), BF),
        V((4, HALF, BLK), BF), V((4, HALF, BLK), BF), V((6 * SETS, PART, BLK), BF), V((HALF, BLK), BF),
        V((SETS, NY - 2, PIECE, BLK), BF), V((SETS, PIECE, BLK), BF), V((SETS, PIECE, BLK), BF), V((1, 128), F32), V((NY, NX, NC, 1, 128), F32),
        V((NZ, 1, 128), F32), V((BLK, BLK), BF),
        V((BLK, BLK), BF), V((BLK, BLK), BF), V((BLK, BLK), BF), V((BLK, BLK), BF), V((BLK, BLK), BF),
        V((BLK, BLK), F32), V((BLK, BLK), F32), V((2, BLK, BLK), F32), V((4, BLK, BLK), F32), V((BLK, BLK), BF),
        V((N, ROWS, BLK), BF), V((N, ROWS, 1024), BF),
        dma((4,)), dma((8,)), dma((8,)), dma((8,)), dma((12,)), dma((12,)), dma, dma, dma((2,)), dma((4,)),
        dma((2,)), dma((2,)), dma((2,)), dma((2, 2)), dma, dma((8,)), dma, dma, dma, dma((8,)), dma((8,)), dma((4,)), dma((4,)),
    ]
    rows, fresh = pl.pallas_call(
        kernel,
        out_shape=(
            jax.ShapeDtypeStruct((4, ROWS, BLK), BF),
            jax.ShapeDtypeStruct((4, ROWS, 1024), BF),
        ),
        in_specs=[anywhere] * 5,
        out_specs=(anywhere, anywhere),
        scratch_shapes=scratch,
        compiler_params=pltpu.CompilerParams(
            collective_id=1, has_side_effects=True, vmem_limit_bytes=62 * 1024 * 1024
        ),
    )(slot_table, grads, factors[0], inverse_factors[0], probes[0])
    out, nf = pl.pallas_call(
        assemble,
        out_shape=(
            jax.ShapeDtypeStruct((4, ROWS, BLK), BF),
            jax.ShapeDtypeStruct((SLOTS, ROWS, 1024), BF),
        ),
        in_specs=[pl.BlockSpec(memory_space=pltpu.SMEM), vmem, vmem, vmem],
        out_specs=(vmem, vmem),
    )(slot_table, factors[0], rows, fresh)
    return (out.reshape(2, 2, ROWS, BLK), nf[None])


def solution(mesh):
    return jax.shard_map(
        body,
        mesh=mesh,
        in_specs=(
            P("dp", None, None, None, "mp"),
            P("mp", None, "dp", None),
            P("mp", None, "dp", None),
            P("mp", None, "dp", None),
            P("mp", None),
        ),
        out_specs=(P(None, None, "dp", "mp"), P("mp", None, "dp", None)),
        check_vma=False,
    )
```

```python
import functools
import math

import jax
import jax.numpy as jnp
from jax import lax
from jax.experimental import pallas as pl
from jax.experimental.pallas import tpu as pltpu
from jax.sharding import PartitionSpec as P

CLIP_RMS = 0.3
LEARN_RATE = 0.1
EPS_NORM = 1e-06

NX, NY, NC = 4, 8, 2
N = NX * NY * NC
NZ = 8
BLK = 512
HALF = 256
SETS = 2
SET = HALF // SETS
PART = SET // 2
PIECE = SET // NY
ROWS = BLK // N
SLOTS = 8
ENTRIES = 2 * 2 * 512 * 4096

BF = jnp.bfloat16
F32 = jnp.float32
MESH = pl.DeviceIdType.MESH


def dev(y, x, c):
    return (lax.rem(y + NY, NY) * NX + lax.rem(x + NX, NX)) * NC + c


def width(q):
    return BLK - 128 * q


def owner_of(b, k):
    return ((2 + 4 * k) * NX + b) * NC


def mm(a, b):
    return jnp.dot(a, b, preferred_element_type=F32)


def mm_nt(a, b):
    return lax.dot_general(a, b, (((1,), (1,)), ((), ())), preferred_element_type=F32)


def mm_tn(a, b):
    return lax.dot_general(a, b, (((0,), (0,)), ((), ())), preferred_element_type=F32)


def kernel(
    t_hbm, g_hbm, f_hbm, v_hbm, p_hbm, out, nf_hbm,
    table, fac, inv, prb, send, relay, recv,
    h, hr, xb, sbuf, yr, y4, pb, sb, sall, zall, gbuf,
    lm, rm, km, hm, vm, ql, qr, pn, mid, wm, res, nf, nfr, full_nf, out_sem,
    load_sem, own_sem, d2d_s, d2d_r, x_s, x_r, rel_s, rel_r, fac_s, fac_r,
    y_s, y_r, y4_r, g_s, g_r, s_s, s_r, z_s, z_r, nf_s, res_s, res_r, nf_r,
):
    i = lax.axis_index("dp")
    z = lax.axis_index("mp")
    c = lax.rem(i, NC)
    x = lax.rem(i // NC, NX)
    y = i // (NC * NX)
    is_owner = (c == 0) & (lax.rem(y, 4) == 2)
    band = y // 2

    def to_owners(src, dst, ssem, rsem):
        for k in range(2):
            goal = dev(2 + 4 * k, x, 0)

            @pl.when(i != goal)
            def _():
                remote(src, dst, ssem.at[k], rsem, goal).start()

            @pl.when(i == goal)
            def _():
                pltpu.make_async_copy(src, dst, rsem).start()

    def owners_sent(src, ssem):
        for k in range(2):

            @pl.when(i != dev(2 + 4 * k, x, 0))
            def _():
                pltpu.make_async_copy(src, src, ssem.at[k]).wait()

    def by_band(fn):
        for q in range(4):
            pl.when(band == q)(functools.partial(fn, q))

    def remote(src, dst, ssem, rsem, d, zz=None):
        return pltpu.make_async_remote_copy(
            src_ref=src, dst_ref=dst, send_sem=ssem, recv_sem=rsem,
            device_id=(d, z if zz is None else zz), device_id_type=MESH,
        )

    def blk(o):
        return lax.rem(x + o, NX)

    loads = [
        pltpu.make_async_copy(t_hbm, table, load_sem.at[3]),
        pltpu.make_async_copy(f_hbm, fac, load_sem.at[0]),
        pltpu.make_async_copy(v_hbm, inv, load_sem.at[1]),
        pltpu.make_async_copy(p_hbm, prb, load_sem.at[2]),
    ]
    for cp in loads:
        cp.start()
    own = {}
    keep = pl.multiple_of(HALF * c, HALF)
    give = pl.multiple_of(HALF * (1 - c), HALF)
    order = ((2, 0), (2, 1), (1, 0), (3, 0), (1, 1), (3, 1), (0, 0), (0, 1))
    for o, s in order:
        own[o, s] = pltpu.make_async_copy(
            g_hbm.at[blk(o), pl.ds(keep + SET * s, SET)], h.at[blk(o), pl.ds(SET * s, SET)], own_sem.at[2 * o + s]
        )
        own[o, s].start()

    bar = pltpu.get_barrier_semaphore()
    sib = dev(y, x, 1 - c)
    right, left = dev(y, x + 1, c), dev(y, x - 1, c)
    for d in [sib, right, left, dev(y, x + 2, c)] + [dev(y + k, x, c) for k in range(1, NY)]:
        pl.semaphore_signal(bar, inc=1, device_id=(d, z), device_id_type=MESH)

    @pl.when(is_owner)
    def _():
        for k in range(1, NZ):
            pl.semaphore_signal(bar, inc=1, device_id=(i, lax.rem(z + k, NZ)), device_id_type=MESH)
        pl.semaphore_wait(bar, 11 + NZ - 1)

    @pl.when(jnp.logical_not(is_owner))
    def _():
        pl.semaphore_wait(bar, 11)

    d2d = {}
    for o, s in order:
        d2d[o, s] = remote(
            g_hbm.at[blk(o), pl.ds(give + SET * s, SET)], hr.at[blk(o), pl.ds(SET * s, SET)],
            d2d_s.at[2 * o + s], d2d_r.at[2 * o + s], sib,
        )
        d2d[o, s].start()

    for cp in loads:
        cp.wait()

    def pack(q):
        w = width(q)
        total = 4 * w + BLK
        for b in range(NX):
            j = table[0, b]
            for k, src in ((0, fac), (1, fac), (2, inv), (3, inv)):
                lo = BLK * (k % 2)
                send[b, :, k * w : (k + 1) * w] = src[j, :, lo + BLK - w : lo + BLK]
            send[b, :, 4 * w : total] = prb[j]
        for k in (1, 3, 2):
            to = blk(k)
            remote(
                send.at[to, :, pl.ds(0, total)], relay.at[x, :, pl.ds(0, total)],
                rel_s, rel_r, dev(y, x + k, c),
            ).start()
        relay[x, :, 0:total] = send[x, :, 0:total]

    by_band(pack)

    def forward(q):
        total = 4 * width(q) + BLK
        three = relay.at[pl.ds(0, 3), :, pl.ds(0, total)]
        pltpu.make_async_copy(three, three, rel_r).wait()
        src = relay.at[:, :, pl.ds(0, total)]
        dst = recv.at[y, :, c, :, pl.ds(0, total)]

        to_owners(src, dst, fac_s, fac_r.at[q])

    def merge(o, s):
        own[o, s].wait()
        d2d[o, s].wait()
        part = pl.ds(SET * s, SET)
        h[blk(o), part] = (h[blk(o), part].astype(F32) + hr[blk(o), part].astype(F32)).astype(BF)

    def top(s):
        return pl.ds(SET * s, PART)

    def bot(s):
        return pl.ds(SET * s + PART, PART)

    xs = {}

    def xsend(k, s, b, part, d):
        n = 6 * s + k
        xs[k, s] = remote(h.at[b, part], xb.at[n], x_s.at[n], x_r.at[n], d)
        xs[k, s].start()

    def plus(k, s, b, part):
        xs[k, s].wait_recv()
        h[b, part] = (h[b, part].astype(F32) + xb[6 * s + k].astype(F32)).astype(BF)

    for s in range(SETS):
        merge(2, s)
        xsend(0, s, blk(2), top(s), right)
        xsend(1, s, blk(2), bot(s), left)
    merge(1, 0)
    xsend(2, 0, blk(1), bot(0), right)
    merge(3, 0)
    xsend(3, 0, blk(3), top(0), left)
    merge(1, 1)
    merge(3, 1)
    by_band(forward)
    for s in range(SETS):
        plus(0, s, blk(1), top(s))
        xsend(4, s, blk(1), top(s), right)
        plus(1, s, blk(3), bot(s))
        xsend(5, s, blk(3), bot(s), left)
        if s == 0:
            xsend(2, 1, blk(1), bot(1), right)
            xsend(3, 1, blk(3), top(1), left)
    merge(0, 0)
    merge(0, 1)

    def piece(s, k):
        return pl.ds(SET * s + pl.multiple_of(PIECE * lax.rem(y + k, NY), PIECE), PIECE)

    def ysend(s, slot, k):
        remote(sbuf.at[piece(s, k)], yr.at[s, slot], y_s.at[s], y_r.at[s], dev(y + k, x, c)).start()

    for s in range(SETS):
        for k in (2, 3, 4, 5):
            xs[k, s].wait_recv()
        n = 6 * s
        sbuf[top(s)] = (h[x, top(s)].astype(F32) + xb[n + 3].astype(F32) + xb[n + 4].astype(F32)).astype(BF)
        sbuf[bot(s)] = (h[x, bot(s)].astype(F32) + xb[n + 2].astype(F32) + xb[n + 5].astype(F32)).astype(BF)
        if s == 0:
            far = remote(sbuf.at[piece(s, 4)], y4, y_s.at[s], y4_r, dev(y + 7, x, c))
            far.start()
        else:
            ysend(s, 6, 4)
            ysend(s, 5, 5)
        for slot, k in enumerate((3, 6, 2, 7, 1)):
            ysend(s, slot, k)

    far.wait_recv()
    sbuf[piece(0, 5)] = (sbuf[piece(0, 5)].astype(F32) + y4[...].astype(F32)).astype(BF)
    ysend(0, 5, 5)
    for cp in xs.values():
        cp.wait_send()
    sq = jnp.zeros((1, BLK), F32)

    def ysum(s):
        count = NY - 2 + s
        got = yr.at[s, pl.ds(0, count)]
        pltpu.make_async_copy(got, got, y_r.at[s]).wait()
        acc = sbuf[piece(s, 0)].astype(F32)
        for k in range(count):
            acc = acc + yr[s, k].astype(F32)
        pb[s] = acc.astype(BF)
        return jnp.sum(acc * acc, axis=0, keepdims=True)

    def pieces(s):
        mine = pl.ds(pl.multiple_of(HALF * c + SET * s + PIECE * y, PIECE), PIECE)
        to_owners(pb.at[s], gbuf.at[mine], g_s.at[s], g_r)

    sq = ysum(0)
    pieces(0)
    sq = sq + ysum(1)
    sb[...] = sq[:, 0:128] + sq[:, 128:256] + sq[:, 256:384] + sq[:, 384:512]

    for b in range(NX):
        for k in range(2):
            ow = owner_of(b, k)

            @pl.when(i != ow)
            def _():
                remote(sb, sall.at[y, x, c], s_s.at[2 * b + k], s_r, ow).start()

            @pl.when(i == ow)
            def _():
                pltpu.make_async_copy(sb, sall.at[y, x, c], s_r).start()

    pieces(1)

    @pl.when(is_owner)
    def _():
        for m in (lm, rm, km, hm):
            for q in range(1, 4):
                m[128 * q : 128 * (q + 1), 0 : 128 * q] = jnp.zeros((128, 128 * q), BF)
        for q in range(4):
            w = width(q)
            got = recv.at[pl.ds(2 * q, 2), :, :, :, pl.ds(0, 4 * w + BLK)]
            pltpu.make_async_copy(got, got, fac_r.at[q]).wait()
        for q in range(4):
            w = width(q)
            rows = slice(128 * q, 128 * (q + 1))
            for k, m in enumerate((lm, rm, km, hm)):
                part = recv[2 * q : 2 * q + 2, :, :, :, k * w : (k + 1) * w]
                m[rows, BLK - w : BLK] = part.astype(F32).reshape(128, w).astype(BF)
            part = recv[2 * q : 2 * q + 2, :, :, :, 4 * w : 4 * w + BLK]
            vm[rows] = part.astype(F32).reshape(128, BLK).astype(BF)
        row = lax.broadcasted_iota(jnp.int32, (BLK, BLK), 0)
        col = lax.broadcasted_iota(jnp.int32, (BLK, BLK), 1)

        def full(v):
            return jnp.full((1, 1), v, F32)

        def upper(m):
            return jnp.where(row <= col, m, 0.0).astype(BF)

        def scaled(m):
            top_value = jnp.maximum(jnp.max(jnp.abs(m)), 1e-30)
            return (m * (1.0 / full(top_value))).astype(BF), top_value

        wm[...] = mm_tn(km[...], vm[...]).astype(BF)
        wm[...], q_top = scaled(mm(wm[...], hm[...]))
        for side, (m, gram) in enumerate(((lm, mm_nt), (rm, mm_tn))):
            value = gram(wm[...], wm[...])
            (ql, qr)[side][...] = value
            mid[side] = mm(upper(value), m[...])

        pltpu.make_async_copy(sall, sall, s_r).wait()
        zall[z] = jnp.sum(sall[...], axis=(0, 1, 2))
        local = jnp.sum(sall[:, x])

        def tell_z(k, _):
            remote(zall.at[z], zall.at[z], z_s, z_r, i, lax.rem(z + k, NZ)).start()
            return 0

        lax.fori_loop(1, NZ, tell_z, 0)
        limit = CLIP_RMS * math.sqrt(ENTRIES)

        def clip_of(squares):
            return jnp.minimum(1.0, limit * lax.rsqrt(full(squares + EPS_NORM)))

        pltpu.make_async_copy(gbuf, gbuf, g_r).wait()
        first_clip = clip_of(local)
        gbuf[...] = (gbuf[...].astype(F32) * first_clip).astype(BF)
        vm[...] = mm(lm[...], gbuf[...]).astype(BF)
        wm[...], p_top = scaled(mm_nt(vm[...], rm[...]))
        for side, (m, gram) in enumerate(((lm, mm_nt), (rm, mm_tn))):
            value = gram(wm[...], wm[...])
            pn[side] = value
            mid[2 + side] = mm(upper(value), m[...])
        others = zall.at[pl.ds(0, NZ - 1)]
        pltpu.make_async_copy(others, others, z_r).wait()
        ratio = clip_of(jnp.sum(zall[...])) / first_clip
        gbuf[...] = (gbuf[...].astype(F32) * ratio).astype(BF)
        p_scale = (ratio * p_top) * (ratio * p_top)
        q_scale = full(q_top) * full(q_top)
        for side, (m, q_ref, new) in enumerate(((lm, ql, km), (rm, qr, hm))):
            parts = [(slice(128 * q, 128 * (q + 1)), slice(128 * q, BLK)) for q in range(4)]
            tops = [jnp.max(jnp.abs(p_scale * pn[side, r, k] + q_scale * q_ref[r, k])) for r, k in parts]
            bound = functools.reduce(jnp.maximum, tops) + EPS_NORM
            rate = LEARN_RATE / full(bound)
            p_rate, q_rate = rate * p_scale, rate * q_scale
            for r, k in parts:
                moved = p_rate * mid[2 + side, r, k] - q_rate * mid[side, r, k]
                new[r, k] = (m[r, k].astype(F32) - moved).astype(BF)
        for q in range(4):
            w = width(q)
            for k, m in enumerate((km, hm)):
                part = m[128 * q : 128 * (q + 1), BLK - w : BLK]
                nf[16 * q : 16 * (q + 1), :, k * w : (k + 1) * w] = part.astype(F32).reshape(16, ROWS, w).astype(BF)

        def back(src, dst, sems, rsem, widths):
            def refs(d, row):
                w = widths[row // 2]
                return src.at[d, :, pl.ds(0, w)], dst.at[x, :, pl.ds(0, w)]

            def rows_from(base):
                for t in range(NX * NC):
                    for step in (1, -1, 2, -2, 0):
                        row = (base + step) % NY
                        if (step == 2 and t % 2 == 1) or (step == -2 and t % 2 == 0):
                            continue
                        d = NX * NC * row + t
                        if step == 0 and t % 2 == 0:
                            if t == 0:
                                pltpu.make_async_copy(*refs(i, row), rsem.at[x]).start()
                                continue
                            d = dev(row, x + t // 2, 0)
                        remote(*refs(d, row), sems.at[row], rsem.at[x], d).start()

            for base in (2, 6):
                pl.when(y == base)(functools.partial(rows_from, base))

        nf_widths = [2 * width(q) for q in range(4)]
        res_widths = [BLK] * 4
        back(nf, nfr, nf_s, nf_r, nf_widths)
        vm[...] = mm_tn(km[...], km[...]).astype(BF)
        wm[...] = mm_tn(hm[...], hm[...]).astype(BF)
        vm[...] = mm(vm[...], gbuf[...]).astype(BF)
        res[...] = mm(vm[...], wm[...]).reshape(N, ROWS, BLK).astype(BF)

        back(res, out, res_s, res_r, res_widths)

    def landed(q):
        for b in range(NX):
            part = nfr.at[b, :, pl.ds(0, 2 * width(q))]
            pltpu.make_async_copy(part, part, nf_r.at[b]).wait()
        w = width(q)
        for j in range(SLOTS):
            which = jnp.int32(0)
            hit = jnp.int32(0)
            for b in range(NX):
                same = table[0, b] == j
                which = jnp.where(same, b, which)
                hit = jnp.where(same, 1, hit)
            for side in range(2):
                lo = BLK * side
                old = fac[j, :, lo + BLK - w : lo + BLK]
                new = nfr[which, :, side * w : (side + 1) * w]
                full_nf[j, :, lo + BLK - w : lo + BLK] = jnp.where(
                    hit == 1, new.astype(F32), old.astype(F32)
                ).astype(BF)
                if q:
                    full_nf[j, :, lo : lo + BLK - w] = jnp.zeros((ROWS, BLK - w), BF)

    by_band(landed)
    finish = pltpu.make_async_copy(full_nf, nf_hbm, out_sem)
    finish.start()
    for b in range(NX):
        pltpu.make_async_copy(out.at[b], out.at[b], res_r.at[b]).wait()
    finish.wait()

    seven = sbuf.at[pl.ds(0, 7 * PIECE)]
    for s in range(SETS):
        pltpu.make_async_copy(seven, seven, y_s.at[s]).wait()

    def sent(q):
        total = 4 * width(q) + BLK
        three = relay.at[pl.ds(0, 3), :, pl.ds(0, total)]
        pltpu.make_async_copy(three, three, rel_s).wait()

        owners_sent(relay.at[:, :, pl.ds(0, total)], fac_s)

    by_band(sent)
    for s in range(SETS):
        owners_sent(pb.at[s], g_s.at[s])
    for b in range(NX):
        for k in range(2):

            @pl.when(i != owner_of(b, k))
            def _():
                pltpu.make_async_copy(sb, sb, s_s.at[2 * b + k]).wait()

    @pl.when(is_owner)
    def _():
        others = zall.at[pl.ds(0, NZ - 1)]
        pltpu.make_async_copy(others, others, z_s).wait()

        nf_widths = [2 * width(q) for q in range(4)]

        def gone(src, sem, count, w):
            some = src.at[pl.ds(0, count), :, pl.ds(0, w)]
            pltpu.make_async_copy(some, some, sem).wait()

        for yy in range(NY):
            gap = lax.rem(yy + NY - y, NY)
            for count, here in ((7, gap == 0), (8, (gap == 1) | (gap == 7)), (4, (gap == 2) | (gap == 6))):

                @pl.when(here)
                def _():
                    gone(nf, nf_s.at[yy], count, nf_widths[yy // 2])
                    gone(res, res_s.at[yy], count, BLK)


def hand_on(rows_in, nf_in, rows_out, nf_out, rows, nf, sems):
    ins = [pltpu.make_async_copy(nf_in, nf, sems.at[0]), pltpu.make_async_copy(rows_in, rows, sems.at[1])]
    outs = [pltpu.make_async_copy(nf, nf_out, sems.at[2]), pltpu.make_async_copy(rows, rows_out, sems.at[3])]
    for cp in ins:
        cp.start()
    for first, second in zip(ins, outs):
        first.wait()
        second.start()
    for cp in outs:
        cp.wait()


def body(partial_grads, factors, inverse_factors, probes, slot_table):
    grads = partial_grads.reshape(4, BLK, BLK)
    anywhere = pl.BlockSpec(memory_space=pl.ANY)
    dma = pltpu.SemaphoreType.DMA
    V = pltpu.VMEM
    scratch = [
        pltpu.SMEM((1, 4), jnp.int32),
        V((SLOTS, ROWS, 1024), BF), V((SLOTS, ROWS, 1024), BF), V((SLOTS, ROWS, 512), BF),
        V((4, ROWS, 2560), BF), V((4, ROWS, 2560), BF), V((NY, NX, NC, ROWS, 2560), BF),
        V((4, HALF, BLK), BF), V((4, HALF, BLK), BF), V((6 * SETS, PART, BLK), BF), V((HALF, BLK), BF),
        V((SETS, NY - 1, PIECE, BLK), BF), V((PIECE, BLK), BF), V((SETS, PIECE, BLK), BF), V((1, 128), F32), V((NY, NX, NC, 1, 128), F32),
        V((NZ, 1, 128), F32), V((BLK, BLK), BF),
        V((BLK, BLK), BF), V((BLK, BLK), BF), V((BLK, BLK), BF), V((BLK, BLK), BF), V((BLK, BLK), BF),
        V((BLK, BLK), F32), V((BLK, BLK), F32), V((2, BLK, BLK), F32), V((4, BLK, BLK), F32), V((BLK, BLK), BF),
        V((N, ROWS, BLK), BF), V((N, ROWS, 1024), BF), V((4, ROWS, 1024), BF), V((SLOTS, ROWS, 1024), BF), dma,
        dma((4,)), dma((8,)), dma((8,)), dma((8,)), dma((12,)), dma((12,)), dma, dma, dma((2,)), dma((4,)),
        dma((2,)), dma((2,)), dma, dma((2, 2)), dma, dma((8,)), dma, dma, dma, dma((8,)), dma((8,)), dma((4,)), dma((4,)),
    ]
    shapes = (
        jax.ShapeDtypeStruct((4, ROWS, BLK), BF),
        jax.ShapeDtypeStruct((SLOTS, ROWS, 1024), BF),
    )
    rows, fresh = pl.pallas_call(
        kernel,
        out_shape=shapes,
        in_specs=[anywhere] * 5,
        out_specs=(anywhere, anywhere),
        scratch_shapes=scratch,
        compiler_params=pltpu.CompilerParams(
            collective_id=1, has_side_effects=True, vmem_limit_bytes=62 * 1024 * 1024
        ),
    )(slot_table, grads, factors[0], inverse_factors[0], probes[0])
    out, nf = pl.pallas_call(
        hand_on,
        out_shape=shapes,
        in_specs=[anywhere] * 2,
        out_specs=(anywhere, anywhere),
        scratch_shapes=[V((4, ROWS, BLK), BF), V((SLOTS, ROWS, 1024), BF), dma((4,))],
    )(rows, fresh)
    return (out.reshape(2, 2, ROWS, BLK), nf[None])


def solution(mesh):
    return jax.shard_map(
        body,
        mesh=mesh,
        in_specs=(
            P("dp", None, None, None, "mp"),
            P("mp", None, "dp", None),
            P("mp", None, "dp", None),
            P("mp", None, "dp", None),
            P("mp", None),
        ),
        out_specs=(P(None, None, "dp", "mp"), P("mp", None, "dp", None)),
        check_vma=False,
    )
```

```python
import functools
import math

import jax
import jax.numpy as jnp
from jax import lax
from jax.experimental import pallas as pl
from jax.experimental.pallas import tpu as pltpu
from jax.sharding import PartitionSpec as P

CLIP_RMS = 0.3
LEARN_RATE = 0.1
EPS_NORM = 1e-06

NX, NY, NC = 4, 8, 2
N = NX * NY * NC
NZ = 8
BLK = 512
HALF = 256
SETS = 2
SET = HALF // SETS
PART = SET // 2
PIECE = SET // NY
ROWS = BLK // N
SLOTS = 8
ENTRIES = 2 * 2 * 512 * 4096

BF = jnp.bfloat16
F32 = jnp.float32
MESH = pl.DeviceIdType.MESH


def dev(y, x, c):
    return (lax.rem(y + NY, NY) * NX + lax.rem(x + NX, NX)) * NC + c


def width(q):
    return BLK - 128 * q


def owner_of(b, k):
    return ((2 + 4 * k) * NX + b) * NC


def mm(a, b):
    return jnp.dot(a, b, preferred_element_type=F32)


def mm_nt(a, b):
    return lax.dot_general(a, b, (((1,), (1,)), ((), ())), preferred_element_type=F32)


def mm_tn(a, b):
    return lax.dot_general(a, b, (((0,), (0,)), ((), ())), preferred_element_type=F32)


def kernel(
    t_hbm, g_hbm, f_hbm, v_hbm, p_hbm, out, nf_hbm,
    table, fac, inv, prb, send, relay, recv,
    h, hr, xb, sbuf, yr, y4, pb, sb, sall, zall, gbuf,
    lm, rm, km, hm, vm, ql, qr, pn, mid, wm, res, nf, nfr, full_nf, out_sem,
    load_sem, own_sem, d2d_s, d2d_r, x_s, x_r, rel_s, rel_r, fac_s, fac_r,
    y_s, y_r, y4_r, g_s, g_r, s_s, s_r, z_s, z_r, nf_s, res_s, res_r, nf_r,
):
    i = lax.axis_index("dp")
    z = lax.axis_index("mp")
    c = lax.rem(i, NC)
    x = lax.rem(i // NC, NX)
    y = i // (NC * NX)
    is_owner = (c == 0) & (lax.rem(y, 4) == 2)
    band = y // 2

    def to_owners(src, dst, ssem, rsem):
        for k in range(2):
            goal = dev(2 + 4 * k, x, 0)

            @pl.when(i != goal)
            def _():
                remote(src, dst, ssem.at[k], rsem, goal).start()

            @pl.when(i == goal)
            def _():
                pltpu.make_async_copy(src, dst, rsem).start()

    def owners_sent(src, ssem):
        for k in range(2):

            @pl.when(i != dev(2 + 4 * k, x, 0))
            def _():
                pltpu.make_async_copy(src, src, ssem.at[k]).wait()

    def by_band(fn):
        for q in range(4):
            pl.when(band == q)(functools.partial(fn, q))

    def remote(src, dst, ssem, rsem, d, zz=None):
        return pltpu.make_async_remote_copy(
            src_ref=src, dst_ref=dst, send_sem=ssem, recv_sem=rsem,
            device_id=(d, z if zz is None else zz), device_id_type=MESH,
        )

    def blk(o):
        return lax.rem(x + o, NX)

    loads = [
        pltpu.make_async_copy(t_hbm, table, load_sem.at[3]),
        pltpu.make_async_copy(f_hbm, fac, load_sem.at[0]),
        pltpu.make_async_copy(v_hbm, inv, load_sem.at[1]),
        pltpu.make_async_copy(p_hbm, prb, load_sem.at[2]),
    ]
    for cp in loads:
        cp.start()
    own = {}
    keep = pl.multiple_of(HALF * c, HALF)
    give = pl.multiple_of(HALF * (1 - c), HALF)
    order = ((2, 0), (2, 1), (1, 0), (3, 0), (1, 1), (3, 1), (0, 0), (0, 1))
    for o, s in order:
        own[o, s] = pltpu.make_async_copy(
            g_hbm.at[blk(o), pl.ds(keep + SET * s, SET)], h.at[blk(o), pl.ds(SET * s, SET)], own_sem.at[2 * o + s]
        )
        own[o, s].start()

    bar = pltpu.get_barrier_semaphore()
    sib = dev(y, x, 1 - c)
    right, left = dev(y, x + 1, c), dev(y, x - 1, c)
    for d in [sib, right, left, dev(y, x + 2, c)] + [dev(y + k, x, c) for k in range(1, NY)]:
        pl.semaphore_signal(bar, inc=1, device_id=(d, z), device_id_type=MESH)

    @pl.when(is_owner)
    def _():
        for k in range(1, NZ):
            pl.semaphore_signal(bar, inc=1, device_id=(i, lax.rem(z + k, NZ)), device_id_type=MESH)
        pl.semaphore_wait(bar, 11 + NZ - 1)

    @pl.when(jnp.logical_not(is_owner))
    def _():
        pl.semaphore_wait(bar, 11)

    d2d = {}
    for o, s in order:
        d2d[o, s] = remote(
            g_hbm.at[blk(o), pl.ds(give + SET * s, SET)], hr.at[blk(o), pl.ds(SET * s, SET)],
            d2d_s.at[2 * o + s], d2d_r.at[2 * o + s], sib,
        )
        d2d[o, s].start()

    for cp in loads:
        cp.wait()

    def pack(q):
        w = width(q)
        total = 4 * w + BLK
        for b in range(NX):
            j = table[0, b]
            for k, src in ((0, fac), (1, fac), (2, inv), (3, inv)):
                lo = BLK * (k % 2)
                send[b, :, k * w : (k + 1) * w] = src[j, :, lo + BLK - w : lo + BLK]
            send[b, :, 4 * w : total] = prb[j]
        for k in (1, 3, 2):
            to = blk(k)
            remote(
                send.at[to, :, pl.ds(0, total)], relay.at[x, :, pl.ds(0, total)],
                rel_s, rel_r, dev(y, x + k, c),
            ).start()
        relay[x, :, 0:total] = send[x, :, 0:total]

    by_band(pack)

    def forward(q):
        total = 4 * width(q) + BLK
        three = relay.at[pl.ds(0, 3), :, pl.ds(0, total)]
        pltpu.make_async_copy(three, three, rel_r).wait()
        src = relay.at[:, :, pl.ds(0, total)]
        dst = recv.at[y, :, c, :, pl.ds(0, total)]

        to_owners(src, dst, fac_s, fac_r.at[q])

    def merge(o, s):
        own[o, s].wait()
        d2d[o, s].wait()
        part = pl.ds(SET * s, SET)
        h[blk(o), part] = (h[blk(o), part].astype(F32) + hr[blk(o), part].astype(F32)).astype(BF)

    def top(s):
        return pl.ds(SET * s, PART)

    def bot(s):
        return pl.ds(SET * s + PART, PART)

    xs = {}

    def xsend(k, s, b, part, d):
        n = 6 * s + k
        xs[k, s] = remote(h.at[b, part], xb.at[n], x_s.at[n], x_r.at[n], d)
        xs[k, s].start()

    def plus(k, s, b, part):
        xs[k, s].wait_recv()
        h[b, part] = (h[b, part].astype(F32) + xb[6 * s + k].astype(F32)).astype(BF)

    for s in range(SETS):
        merge(2, s)
        xsend(0, s, blk(2), top(s), right)
        xsend(1, s, blk(2), bot(s), left)
    merge(1, 0)
    xsend(2, 0, blk(1), bot(0), right)
    merge(3, 0)
    xsend(3, 0, blk(3), top(0), left)
    merge(1, 1)
    merge(3, 1)
    by_band(forward)
    for s in range(SETS):
        plus(0, s, blk(1), top(s))
        xsend(4, s, blk(1), top(s), right)
        plus(1, s, blk(3), bot(s))
        xsend(5, s, blk(3), bot(s), left)
        if s == 0:
            xsend(2, 1, blk(1), bot(1), right)
            xsend(3, 1, blk(3), top(1), left)
    merge(0, 0)
    merge(0, 1)

    def piece(s, k):
        return pl.ds(SET * s + pl.multiple_of(PIECE * lax.rem(y + k, NY), PIECE), PIECE)

    def ysend(s, slot, k):
        remote(sbuf.at[piece(s, k)], yr.at[s, slot], y_s.at[s], y_r.at[s], dev(y + k, x, c)).start()

    for s in range(SETS):
        for k in (2, 3, 4, 5):
            xs[k, s].wait_recv()
        n = 6 * s
        sbuf[top(s)] = (h[x, top(s)].astype(F32) + xb[n + 3].astype(F32) + xb[n + 4].astype(F32)).astype(BF)
        sbuf[bot(s)] = (h[x, bot(s)].astype(F32) + xb[n + 2].astype(F32) + xb[n + 5].astype(F32)).astype(BF)
        if s == 0:
            far = remote(sbuf.at[piece(s, 4)], y4, y_s.at[s], y4_r, dev(y + 7, x, c))
            far.start()
        else:
            ysend(s, 6, 4)
            ysend(s, 5, 5)
        for slot, k in enumerate((3, 6, 2, 7, 1)):
            ysend(s, slot, k)

    far.wait_recv()
    sbuf[piece(0, 5)] = (sbuf[piece(0, 5)].astype(F32) + y4[...].astype(F32)).astype(BF)
    ysend(0, 5, 5)
    for cp in xs.values():
        cp.wait_send()
    sq = jnp.zeros((1, BLK), F32)

    def ysum(s):
        count = NY - 2 + s
        got = yr.at[s, pl.ds(0, count)]
        pltpu.make_async_copy(got, got, y_r.at[s]).wait()
        acc = sbuf[piece(s, 0)].astype(F32)
        for k in range(count):
            acc = acc + yr[s, k].astype(F32)
        pb[s] = acc.astype(BF)
        return jnp.sum(acc * acc, axis=0, keepdims=True)

    def pieces(s):
        mine = pl.ds(pl.multiple_of(HALF * c + SET * s + PIECE * y, PIECE), PIECE)
        to_owners(pb.at[s], gbuf.at[mine], g_s.at[s], g_r)

    sq = ysum(0)
    pieces(0)
    sq = sq + ysum(1)
    sb[...] = sq[:, 0:128] + sq[:, 128:256] + sq[:, 256:384] + sq[:, 384:512]

    for b in range(NX):
        for k in range(2):
            ow = owner_of(b, k)

            @pl.when(i != ow)
            def _():
                remote(sb, sall.at[y, x, c], s_s.at[2 * b + k], s_r, ow).start()

            @pl.when(i == ow)
            def _():
                pltpu.make_async_copy(sb, sall.at[y, x, c], s_r).start()

    pieces(1)

    @pl.when(is_owner)
    def _():
        for m in (lm, rm, km, hm):
            for q in range(1, 4):
                m[128 * q : 128 * (q + 1), 0 : 128 * q] = jnp.zeros((128, 128 * q), BF)
        for q in range(4):
            w = width(q)
            got = recv.at[pl.ds(2 * q, 2), :, :, :, pl.ds(0, 4 * w + BLK)]
            pltpu.make_async_copy(got, got, fac_r.at[q]).wait()
        for q in range(4):
            w = width(q)
            rows = slice(128 * q, 128 * (q + 1))
            for k, m in enumerate((lm, rm, km, hm)):
                part = recv[2 * q : 2 * q + 2, :, :, :, k * w : (k + 1) * w]
                m[rows, BLK - w : BLK] = part.astype(F32).reshape(128, w).astype(BF)
            part = recv[2 * q : 2 * q + 2, :, :, :, 4 * w : 4 * w + BLK]
            vm[rows] = part.astype(F32).reshape(128, BLK).astype(BF)
        row = lax.broadcasted_iota(jnp.int32, (BLK, BLK), 0)
        col = lax.broadcasted_iota(jnp.int32, (BLK, BLK), 1)

        def full(v):
            return jnp.full((1, 1), v, F32)

        def upper(m):
            return jnp.where(row <= col, m, 0.0).astype(BF)

        def scaled(m):
            top_value = jnp.maximum(jnp.max(jnp.abs(m)), 1e-30)
            return (m * (1.0 / full(top_value))).astype(BF), top_value

        wm[...] = mm_tn(km[...], vm[...]).astype(BF)
        wm[...], q_top = scaled(mm(wm[...], hm[...]))
        for side, (m, gram) in enumerate(((lm, mm_nt), (rm, mm_tn))):
            value = gram(wm[...], wm[...])
            (ql, qr)[side][...] = value
            mid[side] = mm(upper(value), m[...])

        pltpu.make_async_copy(sall, sall, s_r).wait()
        zall[z] = jnp.sum(sall[...], axis=(0, 1, 2))
        local = jnp.sum(sall[:, x])

        for k in (4, 3, 5, 2, 6, 1, 7):
            remote(zall.at[z], zall.at[z], z_s, z_r, i, lax.rem(z + k, NZ)).start()
        limit = CLIP_RMS * math.sqrt(ENTRIES)

        def clip_of(squares):
            return jnp.minimum(1.0, limit * lax.rsqrt(full(squares + EPS_NORM)))

        pltpu.make_async_copy(gbuf, gbuf, g_r).wait()
        first_clip = clip_of(local)
        gbuf[...] = (gbuf[...].astype(F32) * first_clip).astype(BF)
        vm[...] = mm(lm[...], gbuf[...]).astype(BF)
        wm[...], p_top = scaled(mm_nt(vm[...], rm[...]))
        for side, (m, gram) in enumerate(((lm, mm_nt), (rm, mm_tn))):
            value = gram(wm[...], wm[...])
            pn[side] = value
            mid[2 + side] = mm(upper(value), m[...])
        others = zall.at[pl.ds(0, NZ - 1)]
        pltpu.make_async_copy(others, others, z_r).wait()
        ratio = clip_of(jnp.sum(zall[...])) / first_clip
        gbuf[...] = (gbuf[...].astype(F32) * ratio).astype(BF)
        p_scale = (ratio * p_top) * (ratio * p_top)
        q_scale = full(q_top) * full(q_top)
        for side, (m, q_ref, new) in enumerate(((lm, ql, km), (rm, qr, hm))):
            parts = [(slice(128 * q, 128 * (q + 1)), slice(128 * q, BLK)) for q in range(4)]
            tops = [jnp.max(jnp.abs(p_scale * pn[side, r, k] + q_scale * q_ref[r, k])) for r, k in parts]
            bound = functools.reduce(jnp.maximum, tops) + EPS_NORM
            rate = LEARN_RATE / full(bound)
            p_rate, q_rate = rate * p_scale, rate * q_scale
            for r, k in parts:
                moved = p_rate * mid[2 + side, r, k] - q_rate * mid[side, r, k]
                new[r, k] = (m[r, k].astype(F32) - moved).astype(BF)
        for q in range(4):
            w = width(q)
            for k, m in enumerate((km, hm)):
                part = m[128 * q : 128 * (q + 1), BLK - w : BLK]
                nf[16 * q : 16 * (q + 1), :, k * w : (k + 1) * w] = part.astype(F32).reshape(16, ROWS, w).astype(BF)

        def back(src, dst, sems, rsem, widths):
            def refs(d, row):
                w = widths[row // 2]
                return src.at[d, :, pl.ds(0, w)], dst.at[x, :, pl.ds(0, w)]

            def rows_from(base):
                for t in range(NX * NC):
                    for step in (1, -1, 2, -2, 0):
                        row = (base + step) % NY
                        if (step == 2 and t % 2 == 1) or (step == -2 and t % 2 == 0):
                            continue
                        d = NX * NC * row + t
                        if step == 0 and t % 2 == 0:
                            if t == 0:
                                pltpu.make_async_copy(*refs(i, row), rsem.at[x]).start()
                                continue
                            d = dev(row, x + t // 2, 0)
                        remote(*refs(d, row), sems.at[row], rsem.at[x], d).start()

            for base in (2, 6):
                pl.when(y == base)(functools.partial(rows_from, base))

        nf_widths = [2 * width(q) for q in range(4)]
        res_widths = [BLK] * 4
        back(nf, nfr, nf_s, nf_r, nf_widths)
        lo, hi = slice(0, HALF), slice(HALF, BLK)
        for new, dst in ((km, vm), (hm, wm)):
            dst[lo, :] = mm_tn(new[lo, lo], new[lo, :]).astype(BF)
            dst[hi, lo] = mm_tn(new[lo, hi], new[lo, lo]).astype(BF)
            dst[hi, hi] = mm_tn(new[:, hi], new[:, hi]).astype(BF)
        vm[...] = mm(vm[...], gbuf[...]).astype(BF)
        res[...] = mm(vm[...], wm[...]).reshape(N, ROWS, BLK).astype(BF)

        back(res, out, res_s, res_r, res_widths)

    def landed(q):
        for b in range(NX):
            part = nfr.at[b, :, pl.ds(0, 2 * width(q))]
            pltpu.make_async_copy(part, part, nf_r.at[b]).wait()
        w = width(q)
        for j in range(SLOTS):
            which = jnp.int32(0)
            hit = jnp.int32(0)
            for b in range(NX):
                same = table[0, b] == j
                which = jnp.where(same, b, which)
                hit = jnp.where(same, 1, hit)
            for side in range(2):
                lo = BLK * side
                old = fac[j, :, lo + BLK - w : lo + BLK]
                new = nfr[which, :, side * w : (side + 1) * w]
                full_nf[j, :, lo + BLK - w : lo + BLK] = jnp.where(
                    hit == 1, new.astype(F32), old.astype(F32)
                ).astype(BF)
                if q:
                    full_nf[j, :, lo : lo + BLK - w] = jnp.zeros((ROWS, BLK - w), BF)

    by_band(landed)
    finish = pltpu.make_async_copy(full_nf, nf_hbm, out_sem)
    finish.start()
    for b in range(NX):
        pltpu.make_async_copy(out.at[b], out.at[b], res_r.at[b]).wait()
    finish.wait()

    seven = sbuf.at[pl.ds(0, 7 * PIECE)]
    for s in range(SETS):
        pltpu.make_async_copy(seven, seven, y_s.at[s]).wait()

    def sent(q):
        total = 4 * width(q) + BLK
        three = relay.at[pl.ds(0, 3), :, pl.ds(0, total)]
        pltpu.make_async_copy(three, three, rel_s).wait()

        owners_sent(relay.at[:, :, pl.ds(0, total)], fac_s)

    by_band(sent)
    for s in range(SETS):
        owners_sent(pb.at[s], g_s.at[s])
    for b in range(NX):
        for k in range(2):

            @pl.when(i != owner_of(b, k))
            def _():
                pltpu.make_async_copy(sb, sb, s_s.at[2 * b + k]).wait()

    @pl.when(is_owner)
    def _():
        others = zall.at[pl.ds(0, NZ - 1)]
        pltpu.make_async_copy(others, others, z_s).wait()

        nf_widths = [2 * width(q) for q in range(4)]

        def gone(src, sem, count, w):
            some = src.at[pl.ds(0, count), :, pl.ds(0, w)]
            pltpu.make_async_copy(some, some, sem).wait()

        for yy in range(NY):
            gap = lax.rem(yy + NY - y, NY)
            for count, here in ((7, gap == 0), (8, (gap == 1) | (gap == 7)), (4, (gap == 2) | (gap == 6))):

                @pl.when(here)
                def _():
                    gone(nf, nf_s.at[yy], count, nf_widths[yy // 2])
                    gone(res, res_s.at[yy], count, BLK)


def hand_on(rows_in, nf_in, rows_out, nf_out, rows, nf, sems):
    ins = [pltpu.make_async_copy(nf_in, nf, sems.at[0]), pltpu.make_async_copy(rows_in, rows, sems.at[1])]
    outs = [pltpu.make_async_copy(nf, nf_out, sems.at[2]), pltpu.make_async_copy(rows, rows_out, sems.at[3])]
    for cp in ins:
        cp.start()
    for first, second in zip(ins, outs):
        first.wait()
        second.start()
    for cp in outs:
        cp.wait()


def body(partial_grads, factors, inverse_factors, probes, slot_table):
    grads = partial_grads.reshape(4, BLK, BLK)
    anywhere = pl.BlockSpec(memory_space=pl.ANY)
    dma = pltpu.SemaphoreType.DMA
    V = pltpu.VMEM
    scratch = [
        pltpu.SMEM((1, 4), jnp.int32),
        V((SLOTS, ROWS, 1024), BF), V((SLOTS, ROWS, 1024), BF), V((SLOTS, ROWS, 512), BF),
        V((4, ROWS, 2560), BF), V((4, ROWS, 2560), BF), V((NY, NX, NC, ROWS, 2560), BF),
        V((4, HALF, BLK), BF), V((4, HALF, BLK), BF), V((6 * SETS, PART, BLK), BF), V((HALF, BLK), BF),
        V((SETS, NY - 1, PIECE, BLK), BF), V((PIECE, BLK), BF), V((SETS, PIECE, BLK), BF), V((1, 128), F32), V((NY, NX, NC, 1, 128), F32),
        V((NZ, 1, 128), F32), V((BLK, BLK), BF),
        V((BLK, BLK), BF), V((BLK, BLK), BF), V((BLK, BLK), BF), V((BLK, BLK), BF), V((BLK, BLK), BF),
        V((BLK, BLK), F32), V((BLK, BLK), F32), V((2, BLK, BLK), F32), V((4, BLK, BLK), F32), V((BLK, BLK), BF),
        V((N, ROWS, BLK), BF), V((N, ROWS, 1024), BF), V((4, ROWS, 1024), BF), V((SLOTS, ROWS, 1024), BF), dma,
        dma((4,)), dma((8,)), dma((8,)), dma((8,)), dma((12,)), dma((12,)), dma, dma, dma((2,)), dma((4,)),
        dma((2,)), dma((2,)), dma, dma((2, 2)), dma, dma((8,)), dma, dma, dma, dma((8,)), dma((8,)), dma((4,)), dma((4,)),
    ]
    shapes = (
        jax.ShapeDtypeStruct((4, ROWS, BLK), BF),
        jax.ShapeDtypeStruct((SLOTS, ROWS, 1024), BF),
    )
    rows, fresh = pl.pallas_call(
        kernel,
        out_shape=shapes,
        in_specs=[anywhere] * 5,
        out_specs=(anywhere, anywhere),
        scratch_shapes=scratch,
        compiler_params=pltpu.CompilerParams(
            collective_id=1, has_side_effects=True, vmem_limit_bytes=62 * 1024 * 1024
        ),
    )(slot_table, grads, factors[0], inverse_factors[0], probes[0])
    out, nf = pl.pallas_call(
        hand_on,
        out_shape=shapes,
        in_specs=[anywhere] * 2,
        out_specs=(anywhere, anywhere),
        scratch_shapes=[V((4, ROWS, BLK), BF), V((SLOTS, ROWS, 1024), BF), dma((4,))],
    )(rows, fresh)
    return (out.reshape(2, 2, ROWS, BLK), nf[None])


def solution(mesh):
    return jax.shard_map(
        body,
        mesh=mesh,
        in_specs=(
            P("dp", None, None, None, "mp"),
            P("mp", None, "dp", None),
            P("mp", None, "dp", None),
            P("mp", None, "dp", None),
            P("mp", None),
        ),
        out_specs=(P(None, None, "dp", "mp"), P("mp", None, "dp", None)),
        check_vma=False,
    )
```
